128 devices in a mesh: row: 16 (over x, z), col: 8 (over y, core).
Axes of the slice: x: 4, y: 4, z: 4, core: 2. Of those that a mesh axis runs over, the one named last changes fastest.
Arguments:
- img_learner: bfloat16 [24576, 768], P(('row', 'col')), may hold values from -0.19921875 to 0.19921875
- img_refer: bfloat16 [24576, 768], P(('row', 'col')), may hold values from -0.19921875 to 0.19921875
- txt_learner: bfloat16 [24576, 768], P(('row', 'col')), may hold values from -0.19921875 to 0.19921875
- txt_refer: bfloat16 [24576, 768], P(('row', 'col')), may hold values from -0.19921875 to 0.19921875
- patches: bfloat16 [24576, 16, 768], P(('row', 'col')), may hold values from -6 to 6
- chosen: int32 [12288], P(('row', 'col')), may hold values from 0 to 24575, as said below
- trainer_of: int32 [12288, 1], P(('row', 'col')), may hold values from 0 to 127; in each aligned block of 96 rows (0 to 95, 96 to 191, ...) at most 2 rows name the same one
Outputs:
- learnability: float32 [24576], P(('row', 'col'))
- text_grad: float32 [24576, 768], P(('row', 'col'))
- batches: bfloat16 [32768, 16, 768], P(('row', 'col'))
The draws below stay inside these ranges and needn't reach their ends.
Inputs may be any that keep to these rules, and one draw needn't show every extreme that they name: `chosen`: block k of 96 entries holds distinct pair indices from k * 192 to (k + 1) * 192 - 1. `trainer_of`: trainers are numbered in row+col order; within the 96 entries of one device no trainer appears more than 2 times, a bound that some block reaches.
All inputs are finite; a program needn't handle non-finite values.
Results may differ from the reference program's by a relative error of at most 0.012.
The reference program's roundings to bfloat16 on the way (of `slope`) count: a program that leaves them out, or rounds other values in their place, can miss the bound.
Values may be sent and summed in bfloat16 or wider, within the bound.
A program may use at most 128 MiB of HBM per device.

```python
import math
import jax
import jax.numpy as jnp
import numpy as np
from jax import lax

D = 768
ROWS_DEV = 192
P_SIZE = 16
KEEP = 96
CAP = 2
RECV = 256
PAIRS = 24576
DEVICES = 128


def first_picks(device_key):
    return jax.random.permutation(device_key, ROWS_DEV)[:KEEP]


def draw_chosen(key, part):
    key = jax.random.fold_in(key, 7)
    device_keys = jax.random.split(key, DEVICES)
    choices_made = jax.vmap(first_picks)(device_keys).astype(jnp.int32)
    offsets = (jnp.arange(DEVICES, dtype=jnp.int32) * ROWS_DEV)[:, None]
    return (choices_made + offsets).reshape(-1)


def steps_of(own_key, shape, cuts, smallest, high):
    level = 1.0
    for position, shards_of in cuts:
        steps = jax.random.uniform(jax.random.fold_in(jax.random.fold_in(own_key, 6), position), (shards_of,), jnp.float32, smallest / len(cuts), high / len(cuts))
        level = level * jnp.repeat(jnp.exp(steps), shape[position] // shards_of).reshape((-1,) + (1,) * (len(shape) - 1 - position))
    return level


def shared_out(rng, own, number, rows, number_of, top, reach, slope):
    sequence = jax.random.permutation(rng, number_of)
    packed, common = portions_of(number_of, rows * top, reach, slope, True), portions_of(number_of, rows * top, reach, slope, False)
    places = jnp.arange(number_of)

    def named(tallies, rotation):
        used = int((tallies > 0).sum())
        fixed = max(1, used // 4)
        passed = fixed + (places - fixed + rotation * (used - fixed)) % max(1, number_of - fixed)
        return jnp.zeros((number_of,), jnp.int32).at[sequence[jnp.where(places < fixed, places, passed)]].set(jnp.asarray(tallies, jnp.int32))

    tallies = jnp.where(number % 4 == 0, named(packed, number // 4), named(common, number - number // 4 - 1))
    mixed = jax.random.permutation(jax.random.fold_in(own, 3), number_of)
    donor, sink = mixed[0:number_of // 2 * 2:2], mixed[1:number_of // 2 * 2:2]
    room = jnp.minimum(tallies[donor] - 1, reach - tallies[sink]) // 2
    room = jnp.where((donor == sequence[0]) | (sink == sequence[0]) | (tallies[sink] == 0), 0, jnp.maximum(room, 0))
    passed = jax.random.randint(jax.random.fold_in(own, 4), (number_of // 2,), 0, 1 << 20) % (room + 1)
    tallies = tallies.at[donor].add(-passed).at[sink].add(passed)
    items = jnp.searchsorted(jnp.cumsum(tallies), jnp.arange(rows * top), side="right").astype(jnp.int32)
    grid = items.reshape(top, rows).T
    grid = grid[jax.random.permutation(jax.random.fold_in(own, 1), rows)]
    rotation = jax.random.randint(jax.random.fold_in(own, 2), (rows, 1), 0, top)
    return jnp.take_along_axis(grid, (jnp.arange(top)[None, :] + rotation) % top, axis=1)


def portions_of(amount, total, bound, lean, full):
    weights = [(1 << 20) // math.isqrt(rank ** lean) + 1 for rank in range(1, amount + 1)]
    largest = bound if full else min(bound, max(-(-total // amount), total * weights[0] // sum(weights)))
    least = 1 if total - largest >= amount - 1 else 0
    given, rest = [largest] + [least] * (amount - 1), total - largest - least * (amount - 1)
    while rest > 0:
        free = [i for i in range(1, amount) if given[i] < largest] or [i for i in range(1, amount) if given[i] < bound]
        whole, left = sum([weights[i] for i in free]), rest
        for i in free:
            addition = min(bound - given[i], max(1, left * weights[i] // whole), rest)
            given[i] = given[i] + addition
            rest = rest - addition
    return np.array(given)


def noise(key, shape, scale, limit, cuts=(), kind=jnp.bfloat16):
    array = scale * jax.random.normal(key, shape, jnp.float32)
    if cuts:
        array = array * steps_of(key, shape, cuts, -0.22, 0.18)
    return jnp.clip(array, -limit, limit).astype(kind)


def setup_inputs(seed: int = 0) -> dict:
    splits = jax.random.split(jax.random.key(seed), 8)
    img_learner = noise(splits[0], (PAIRS, D), 0.036, 0.19921875, ((0, 128),))
    img_refer = noise(splits[1], (PAIRS, D), 0.036, 0.19921875, ((0, 128),))
    txt_learner = noise(splits[2], (PAIRS, D), 0.036, 0.19921875, ((0, 128),))
    txt_refer = noise(splits[3], (PAIRS, D), 0.036, 0.19921875, ((0, 128),))
    patches = noise(splits[4], (PAIRS, P_SIZE, D), 1.0, 6.0, ((0, 128),))
    chosen = draw_chosen(jax.random.fold_in(splits[7], 71), 0)
    trainer_of_keys = jax.random.split(jax.random.fold_in(splits[6], 1), (DEVICES * KEEP) // KEEP)
    trainer_of_turns = jax.random.permutation(jax.random.fold_in(splits[6], 3), (DEVICES * KEEP) // KEEP)
    trainer_of = jax.vmap(lambda own, number: shared_out(jax.random.fold_in(splits[6], 2), own, number, KEEP, DEVICES, 1, CAP, 2))(trainer_of_keys, trainer_of_turns).reshape((DEVICES * KEEP, 1))
    return dict(img_learner=img_learner, img_refer=img_refer, txt_learner=txt_learner, txt_refer=txt_refer, patches=patches, chosen=chosen, trainer_of=trainer_of)


SCORE_SHARPNESS = 10.0
SCORE_BIAS = -5.0
EPSILON = 1e-06

def unit_rows(embedding):
    widened = embedding.astype(jnp.float32)
    lengths = jnp.sqrt(lax.optimization_barrier(jnp.sum(widened * widened, axis=1, keepdims=True)) + EPSILON)
    return (widened, lengths, (widened / lengths).astype(jnp.bfloat16))

def reference(img_learner, img_refer, txt_learner, txt_refer, patches, chosen, trainer_of):
    pair_total = ROWS_DEV * DEVICES
    block_rows = ROWS_DEV * 8
    _, _, image_learn = unit_rows(img_learner)
    _, _, image_refer = unit_rows(img_refer)
    text_wide, text_length, student_caption_vectors = unit_rows(txt_learner)
    _, _, teacher_caption_vectors = unit_rows(txt_refer)
    selected = jnp.zeros((pair_total,), jnp.float32).at[chosen].set(1.0)
    columns = jnp.arange(pair_total, dtype=jnp.int32)

    def one_block(running, first_row):
        col_acc, derivative_total = running
        student_batch_lines = lax.dynamic_slice_in_dim(image_learn, first_row, block_rows, 0)
        teacher_batch_lines = lax.dynamic_slice_in_dim(image_refer, first_row, block_rows, 0)
        row_marks = lax.dynamic_slice_in_dim(selected, first_row, block_rows, 0)
        row_ids = first_row + jnp.arange(block_rows, dtype=jnp.int32)
        labels = jnp.where(row_ids[:, None] == columns[None, :], 1.0, -1.0)
        student_pair_scores = SCORE_SHARPNESS * jnp.dot(student_batch_lines, student_caption_vectors.T, preferred_element_type=jnp.float32) + SCORE_BIAS
        teacher_pair_scores = SCORE_SHARPNESS * jnp.dot(teacher_batch_lines, teacher_caption_vectors.T, preferred_element_type=jnp.float32) + SCORE_BIAS
        loss_gaps = jax.nn.softplus(-labels * student_pair_scores) - jax.nn.softplus(-labels * teacher_pair_scores)
        logistic_derivatives = (-labels * jax.nn.sigmoid(-labels * student_pair_scores) * row_marks[:, None] * selected[None, :]).astype(jnp.bfloat16)
        derivative_total = derivative_total + SCORE_SHARPNESS * jnp.dot(logistic_derivatives.T, student_batch_lines, preferred_element_type=jnp.float32)
        return ((col_acc + lax.optimization_barrier(jnp.sum(loss_gaps, axis=0)), derivative_total), lax.optimization_barrier(jnp.sum(loss_gaps, axis=1)))
    starts = jnp.arange(DEVICES // 8, dtype=jnp.int32) * block_rows
    start_state = (jnp.zeros((pair_total,), jnp.float32), jnp.zeros((pair_total, D), jnp.float32))
    (col_sums, grad_sums), row_sums = lax.scan(one_block, start_state, starts)
    learnability = row_sums.reshape(pair_total) + col_sums
    text_grad = grad_sums / text_length - text_wide * (lax.optimization_barrier(jnp.sum(text_wide * grad_sums, axis=1, keepdims=True)) / text_length ** 3)
    owners = trainer_of[:, 0].reshape(DEVICES, KEEP)
    positions = jnp.arange(KEEP, dtype=jnp.int32)
    matches = (owners[:, :, None] == owners[:, None, :]) & (positions[None, None, :] < positions[None, :, None])
    list_ranks = lax.optimization_barrier(jnp.sum(matches.astype(jnp.int32), axis=2))
    sources = jnp.arange(DEVICES, dtype=jnp.int32)[:, None]
    targets = (owners * RECV + sources * CAP + list_ranks).reshape(-1).astype(jnp.int32)
    batches = jnp.zeros((DEVICES * RECV, P_SIZE, D), jnp.bfloat16).at[targets].set(patches[chosen])
    return (learnability, text_grad, batches)
```

```python
import math
import jax
import jax.numpy as jnp
from jax import lax
from jax.experimental import pallas as pl
from jax.experimental.pallas import tpu as pltpu
from jax.sharding import PartitionSpec as P

EPSILON = 1e-06
D = 768
ROWS = 192
HALF = 96
PATCH = 16
DEVICES = 128
MESH = pl.DeviceIdType.MESH
HIGHEST = lax.Precision.HIGHEST
EXP_SCALE = 10.0 * math.log2(math.e)
SHIFT = math.exp(5.0)
GROUP = 6
GROUP_SCALE = math.exp(-5.0 * GROUP)


def patch_order():
    seen = []
    for x in range(4):
        for y in range(4):
            for z in range(4):
                for k in range(2):
                    for p in ((x, y, z), (y, z, x), (z, x, y)):
                        for q in (p, tuple((-v) % 4 for v in p)):
                            o = q + (k,)
                            if any(o) and o not in seen:
                                seen.append(o)
    return seen


def z_of(zh, zl):
    return zl + zh * (3 - 2 * zl)


def device(x, y, z, k):
    return (x * 4 + z, y * 2 + k)


def unit(rows):
    wide = rows.astype(jnp.float32)
    length = jnp.sqrt(jnp.sum(wide * wide, axis=1, keepdims=True) + EPSILON)
    return (wide / length).astype(jnp.bfloat16)


def dot_t(a, b, precision=None):
    return lax.dot_general(
        a, b, (((1,), (1,)), ((), ())), preferred_element_type=jnp.float32, precision=precision
    )


def dot(a, b, precision=None):
    return lax.dot_general(
        a, b, (((1,), (0,)), ((), ())), preferred_element_type=jnp.float32, precision=precision
    )


def product(parts):
    while len(parts) > 1:
        tail = parts[len(parts) // 2 * 2 :]
        parts = [a * b for a, b in zip(parts[0::2], parts[1::2])] + tail
    return parts[0]


def kernel(
    slot_row,
    pos_row,
    pos_col,
    img_l,
    img_r,
    txt_l,
    txt_r,
    patches,
    learn_out,
    grad_out,
    batches,
    texts,
    images,
    pool,
    slots,
    logit_l,
    logit_r,
    slope,
    grads,
    grad_send,
    grad_recv,
    text_acc,
    image_acc,
    text_send,
    text_recv,
    image_send,
    image_recv,
    pool_sem,
    own_sem,
    text_sems,
    image_sems,
    send_sems,
    recv_sems,
):
    row = lax.axis_index("row")
    col = lax.axis_index("col")
    x, z = row // 4, row % 4
    y, k = col // 2, col % 2
    zh = z // 2
    zl = (z + zh) % 2
    me = row * 8 + col
    my_text = x * 2 + zl
    my_image = (y * 2 + zh) * 2 + k

    pool_copy = pltpu.make_async_copy(patches, pool.at[pl.ds(0, ROWS)], pool_sem)
    pool_copy.start()

    barrier = pltpu.get_barrier_semaphore()

    def greet(i, carry):
        other = (me + i) % DEVICES
        pl.semaphore_signal(barrier, inc=1, device_id=(other // 8, other % 8), device_id_type=MESH)
        return carry

    lax.fori_loop(1, DEVICES, greet, 0)

    places = lax.broadcasted_iota(jnp.int32, (ROWS, ROWS), 0)
    order = (places == pos_row[...]).astype(jnp.float32).astype(jnp.bfloat16)

    def ordered(ref):
        return dot(order, unit(ref[...])).astype(jnp.bfloat16)

    text_learn, text_refer = ordered(txt_l), ordered(txt_r)
    image_learn, image_refer = ordered(img_l), ordered(img_r)
    texts[my_text, 0:2] = text_learn.reshape(2, HALF, D)
    texts[my_text, 2:4] = text_refer.reshape(2, HALF, D)
    images[my_image, 0:2] = image_learn.reshape(2, HALF, D)
    images[my_image, 2:4] = image_refer.reshape(2, HALF, D)

    pl.semaphore_wait(barrier, DEVICES - 1)

    def send(buf, sems, slot, half, target, sender):
        part = buf.at[slot, pl.ds(2 * half, 2)]
        pltpu.make_async_remote_copy(
            src_ref=part,
            dst_ref=part,
            send_sem=send_sems.at[sender],
            recv_sem=sems.at[slot, half],
            device_id=target,
            device_id_type=MESH,
        ).start()

    def arrived(buf, sems, slot, half):
        part = buf.at[slot, pl.ds(2 * half, 2)]
        pltpu.make_async_remote_copy(
            src_ref=part,
            dst_ref=part,
            send_sem=send_sems.at[0],
            recv_sem=sems.at[slot, half],
            device_id=(row, col),
            device_id_type=MESH,
        ).wait_recv()

    def text_at(dx, dz):
        return ((x + dx) % 4) * 2 + (zl + dz) % 2

    def image_at(dy, dz, dk=0):
        return (((y + dy) % 4) * 2 + (zh + dz) % 2) * 2 + (k + dk) % 2

    z_text, z_image = z_of(zh, 1 - zl), z_of(1 - zh, zl)
    x_next, x_prev, x_pair = (
        device((x + 1) % 4, y, z, k),
        device((x + 3) % 4, y, z, k),
        device(x, y, z_text, k),
    )
    y_next, y_prev, y_pair = (
        device(x, (y + 1) % 4, z, k),
        device(x, (y + 3) % 4, z, k),
        device(x, y, z_image, k),
    )
    sibling = device(x, y, z, 1 - k)

    def send_text(slot, half, target):
        send(texts, text_sems, slot, half, target, 0)

    def send_image(slot, half, target):
        send(images, image_sems, slot, half, target, 1)

    for half in range(2):
        for target in (x_pair, x_next, x_prev):
            send_text(my_text, half, target)
        for target in (y_pair, y_next, y_prev):
            send_image(my_image, half, target)
    for half in range(2):
        send_image(my_image, half, sibling)

    pool[ROWS] = jnp.zeros((PATCH, D), jnp.bfloat16)
    pool_copy.wait()

    def place(i, carry):
        slots[i] = pool[slot_row[i]]
        return carry

    lax.fori_loop(0, 2 * DEVICES, place, 0)
    own_part = pl.ds(2 * me, 2)
    own_copy = pltpu.make_async_copy(slots.at[own_part], batches.at[own_part], own_sem)
    own_copy.start()

    for half in range(2):
        arrived(texts, text_sems, text_at(0, 1), half)
        send_text(text_at(0, 1), half, x_next)
        send_text(text_at(0, 1), half, x_prev)
        arrived(images, image_sems, image_at(0, 1), half)
        send_image(image_at(0, 1), half, y_next)
        send_image(image_at(0, 1), half, y_prev)
        send_image(image_at(0, 1), half, sibling)
    for half in range(2):
        arrived(texts, text_sems, text_at(3, 0), half)
        arrived(texts, text_sems, text_at(1, 0), half)
        if half == 0:
            send_text(text_at(3, 0), half, x_next)
        else:
            send_text(text_at(1, 0), half, x_prev)
        arrived(images, image_sems, image_at(3, 0), half)
        arrived(images, image_sems, image_at(1, 0), half)
        if half == 0:
            send_image(image_at(3, 0), half, y_next)
        else:
            send_image(image_at(1, 0), half, y_prev)
        send_image(image_at(3, 0), half, sibling)
        send_image(image_at(1, 0), half, sibling)
    for half in range(2):
        arrived(texts, text_sems, text_at(2, 0), half)
        send_text(text_at(2, 0), half, x_pair)
        arrived(images, image_sems, image_at(2, 0), half)
        send_image(image_at(2, 0), half, y_pair)
        send_image(image_at(2, 0), half, sibling)

    for dx, dy, dz, dk in patch_order():
        r = ((x + dx) % 4) * 4 + (z + dz) % 4
        c = ((y + dy) % 4) * 2 + (k + dk) % 2
        pltpu.make_async_remote_copy(
            src_ref=slots.at[pl.ds(2 * (r * 8 + c), 2)],
            dst_ref=batches.at[own_part],
            send_sem=send_sems.at[2],
            recv_sem=recv_sems.at[0],
            device_id=(r, c),
            device_id_type=MESH,
        ).start()

    for half in range(2):
        for dx in (1, 3, 2):
            arrived(texts, text_sems, text_at(dx, 1), half)
        for dy in (1, 3, 2):
            arrived(images, image_sems, image_at(dy, 1), half)
            send_image(image_at(dy, 1), half, sibling)
    for half in range(2):
        for dy in range(4):
            for dz in range(2):
                arrived(images, image_sems, image_at(dy, dz, 1), half)

    text_acc[...] = jnp.zeros_like(text_acc)
    image_acc[...] = jnp.zeros_like(image_acc)

    def pair_tile(step, with_grad):
        text_class = step // 4
        image_class = step // 2 % 2
        image_half = step % 2
        blocks = pl.ds(image_half * 8, 8)
        learn_cols = images[blocks, image_class].reshape(8 * HALF, D)
        logit_l[...] = dot_t(texts[:, text_class].reshape(8 * HALF, D), learn_cols)
        refer_cols = images[blocks, 2 + image_class].reshape(8 * HALF, D)
        logit_r[...] = dot_t(texts[:, 2 + text_class].reshape(8 * HALF, D), refer_cols)

        def one_block(b, total):
            for part in range(2):
                start = pl.multiple_of(b * HALF + part * 48, 16)
                rows = pl.ds(start, 48)
                e_l = jnp.exp2(logit_l[rows, :] * EXP_SCALE)
                e_r = jnp.exp2(logit_r[rows, :] * EXP_SCALE)
                p_l, p_r = e_l + SHIFT, e_r + SHIFT
                if with_grad:
                    slope[rows, :] = (e_l / p_l).astype(jnp.bfloat16)

                def gap(parts_l, parts_r):
                    return jnp.log(product(parts_l) * GROUP_SCALE) - jnp.log(
                        product(parts_r) * GROUP_SCALE
                    )

                across = gap(
                    [p_l[:, 128 * i : 128 * (i + 1)] for i in range(GROUP)],
                    [p_r[:, 128 * i : 128 * (i + 1)] for i in range(GROUP)],
                )
                text_acc[b, text_class, pl.ds(part * 48, 48), :] += across
                total = total + gap(
                    [p_l[8 * i : 8 * (i + 1), :] for i in range(GROUP)],
                    [p_r[8 * i : 8 * (i + 1), :] for i in range(GROUP)],
                )
            return total

        image_acc[image_half, image_class] += lax.fori_loop(
            0, 8, one_block, jnp.zeros((8, 8 * HALF), jnp.float32)
        )
        if with_grad:
            grads[...] += dot(slope[...], learn_cols)

    grads[...] = jnp.zeros_like(grads)

    def with_grad(step, carry):
        pair_tile(step, True)
        return carry

    lax.fori_loop(0, 2, with_grad, 0)

    def to_text_peers(source, landing, sender, receiver):
        for d in range(1, 8):
            slot = (my_text + d) % 8
            pltpu.make_async_remote_copy(
                src_ref=source.at[slot],
                dst_ref=landing.at[my_text],
                send_sem=send_sems.at[sender],
                recv_sem=recv_sems.at[receiver],
                device_id=device(slot // 2, y, z_of(zh, slot % 2), k),
                device_id_type=MESH,
            ).start()

    grad_send[...] = grads[...].reshape(8, HALF, D).astype(jnp.bfloat16)
    to_text_peers(grad_send, grad_recv, 3, 1)

    def without_grad(step, carry):
        pair_tile(step, False)
        return carry

    lax.fori_loop(2, 8, without_grad, 0)

    ones = jnp.ones((8, 128), jnp.float32)
    for b in range(8):
        sums = dot_t(ones, text_acc[b].reshape(ROWS, 128), HIGHEST)
        text_send[b, :, 0:ROWS] = sums[0:1]
    to_text_peers(text_send, text_recv, 4, 2)
    for h in range(2):
        for a in range(2):
            image_send[h, :, pl.ds(a * 768, 768)] = jnp.sum(image_acc[h, a], axis=0, keepdims=True)
    for d in range(1, 16):
        slot = (my_image + d) % 16
        pltpu.make_async_remote_copy(
            src_ref=image_send.at[slot // 8],
            dst_ref=image_recv.at[my_image],
            send_sem=send_sems.at[5],
            recv_sem=recv_sems.at[3],
            device_id=device(x, slot // 4, z_of(slot // 2 % 2, zl), slot % 2),
            device_id_type=MESH,
        ).start()
    text_recv[my_text] = text_send[my_text]
    image_recv[my_image] = image_send[my_image // 8]
    grad_recv[my_text] = grad_send[my_text]

    def all_of(buf, count, sender, receiver):
        part = buf.at[pl.ds(0, count)]
        return pltpu.make_async_remote_copy(
            src_ref=part,
            dst_ref=part,
            send_sem=send_sems.at[sender],
            recv_sem=recv_sems.at[receiver],
            device_id=(row, col),
            device_id_type=MESH,
        )

    own_image = image_learn[0:HALF].astype(jnp.float32)
    cosines = jnp.sum(own_image * text_learn[0:HALF].astype(jnp.float32), axis=1, keepdims=True)
    e = jnp.exp2(cosines * EXP_SCALE)
    as_negative = (e / (e + SHIFT)).astype(jnp.bfloat16).astype(jnp.float32)
    as_positive = -(SHIFT / (e + SHIFT)).astype(jnp.bfloat16).astype(jnp.float32)
    all_of(grad_recv, 7, 3, 1).wait_recv()
    total = (as_positive - as_negative) * own_image
    for b in range(8):
        total = total + grad_recv[b].astype(jnp.float32)
    total = total * 10.0
    own_text = dot(order[0:HALF], txt_l[...])
    length = jnp.sqrt(jnp.sum(own_text * own_text, axis=1, keepdims=True) + EPSILON)
    along = jnp.sum(own_text * total, axis=1, keepdims=True) / (length * length * length)
    result = total / length - own_text * along
    back = (lax.broadcasted_iota(jnp.int32, (ROWS, HALF), 1) == pos_col[...]).astype(jnp.float32)
    grad_out[...] = dot(back, result, HIGHEST)

    diagonal = image_refer.astype(jnp.float32) * text_refer.astype(
        jnp.float32
    ) - image_learn.astype(jnp.float32) * text_learn.astype(jnp.float32)
    score = 20.0 * dot_t(jnp.ones((8, D), jnp.float32), diagonal, HIGHEST)
    all_of(text_recv, 7, 4, 2).wait_recv()
    text_sum = jnp.sum(text_recv[:, :, 0:ROWS], axis=0)
    all_of(image_recv, 15, 5, 3).wait_recv()
    image_sum = jnp.sum(image_recv[...], axis=0)
    wanted = lax.broadcasted_iota(jnp.int32, (768, ROWS), 0)
    place_of = lax.broadcasted_iota(jnp.int32, (768, ROWS), 1)
    base = (my_image % 8) * HALF
    pick_sel = (wanted - base == place_of).astype(jnp.float32)
    pick_uns = ((wanted - base + HALF == place_of) & (place_of >= HALF)).astype(jnp.float32)
    pick_sel = jnp.where(place_of < HALF, pick_sel, 0.0)
    rows8 = lambda v: jnp.broadcast_to(v, (8, v.shape[1]))
    score = score + rows8(text_sum)
    score = score + dot(rows8(image_sum[:, 0:768]), pick_sel, HIGHEST)
    score = score + dot(rows8(image_sum[:, 768:1536]), pick_uns, HIGHEST)
    learn_out[...] = dot(score, order.astype(jnp.float32), HIGHEST)[0:1]

    all_of(slots, 2 * (DEVICES - 1), 2, 0).wait_send()
    own_copy.wait()
    all_of(texts, 7, 0, 0).wait_send()
    all_of(images, 15, 1, 0).wait_send()
    all_of(grad_send, 7, 3, 1).wait_send()
    all_of(text_send, 7, 4, 2).wait_send()
    all_of(image_recv, 15, 5, 3).wait_send()
    all_of(batches, 2 * (DEVICES - 1), 2, 0).wait_recv()


def on_device(img_learner, img_refer, txt_learner, txt_refer, patches, chosen, trainer_of):
    flat = lax.axis_index("row") * lax.axis_size("col") + lax.axis_index("col")
    offsets = chosen - flat * ROWS
    rows = jnp.arange(ROWS, dtype=jnp.int32)
    entries = jnp.arange(HALF, dtype=jnp.int32)
    hits = offsets[:, None] == rows[None, :]
    selected = jnp.any(hits, axis=0)
    as_selected = jnp.sum(jnp.where(hits, entries[:, None], 0), axis=0)
    before = jnp.sum(((rows[:, None] < rows[None, :]) & ~selected[:, None]).astype(jnp.int32), axis=0)
    position = jnp.where(selected, as_selected, HALF + before).astype(jnp.int32)
    owners = trainer_of[:, 0]
    earlier = (owners[:, None] == owners[None, :]) & (entries[None, :] < entries[:, None])
    targets = 2 * owners + jnp.sum(earlier.astype(jnp.int32), axis=1)
    wanted = targets[:, None] == jnp.arange(2 * DEVICES, dtype=jnp.int32)[None, :]
    slot_row = ROWS + jnp.sum(jnp.where(wanted, offsets[:, None] - ROWS, 0), axis=0)

    vmem = pl.BlockSpec(memory_space=pltpu.VMEM)
    anywhere = pl.BlockSpec(memory_space=pl.ANY)
    bf16, f32 = jnp.bfloat16, jnp.float32
    learnability, text_grad, batches = pl.pallas_call(
        kernel,
        out_shape=(
            jax.ShapeDtypeStruct((1, ROWS), f32),
            jax.ShapeDtypeStruct((ROWS, D), f32),
            jax.ShapeDtypeStruct((2 * DEVICES, PATCH, D), bf16),
        ),
        in_specs=[pl.BlockSpec(memory_space=pltpu.SMEM)] + [vmem] * 6 + [anywhere],
        out_specs=(vmem, vmem, anywhere),
        scratch_shapes=[
            pltpu.VMEM((8, 4, HALF, D), bf16),
            pltpu.VMEM((16, 4, HALF, D), bf16),
            pltpu.VMEM((ROWS + 1, PATCH, D), bf16),
            pltpu.VMEM((2 * DEVICES, PATCH, D), bf16),
            pltpu.VMEM((8 * HALF, 8 * HALF), f32),
            pltpu.VMEM((8 * HALF, 8 * HALF), f32),
            pltpu.VMEM((8 * HALF, 8 * HALF), bf16),
            pltpu.VMEM((8 * HALF, D), f32),
            pltpu.VMEM((8, HALF, D), bf16),
            pltpu.VMEM((8, HALF, D), bf16),
            pltpu.VMEM((8, 2, HALF, 128), f32),
            pltpu.VMEM((2, 2, 8, 8 * HALF), f32),
            pltpu.VMEM((8, 1, 256), f32),
            pltpu.VMEM((8, 1, 256), f32),
            pltpu.VMEM((2, 1, 1536), f32),
            pltpu.VMEM((16, 1, 1536), f32),
            pltpu.SemaphoreType.DMA,
            pltpu.SemaphoreType.DMA,
            pltpu.SemaphoreType.DMA((8, 2)),
            pltpu.SemaphoreType.DMA((16, 2)),
            pltpu.SemaphoreType.DMA((6,)),
            pltpu.SemaphoreType.DMA((4,)),
        ],
        compiler_params=pltpu.CompilerParams(
            collective_id=0, has_side_effects=True, vmem_limit_bytes=60 * 1024 * 1024
        ),
        name="jest",
    )(
        slot_row,
        position[None, :],
        position[:, None],
        img_learner,
        img_refer,
        txt_learner,
        txt_refer,
        patches,
    )
    return (learnability[0], text_grad, batches)


def solution(mesh):
    placed = (
        P(("row", "col"), None),
        P(("row", "col"), None),
        P(("row", "col"), None),
        P(("row", "col"), None),
        P(("row", "col"), None, None),
        P(("row", "col")),
        P(("row", "col"), None),
    )
    return jax.shard_map(
        on_device,
        mesh=mesh,
        in_specs=placed,
        out_specs=(P(("row", "col")), P(("row", "col"), None), P(("row", "col"), None, None)),
        check_vma=False,
    )
```

```python
import math
import jax
import jax.numpy as jnp
from jax import lax
from jax.experimental import pallas as pl
from jax.experimental.pallas import tpu as pltpu
from jax.sharding import PartitionSpec as P

EPSILON = 1e-06
D = 768
ROWS = 192
HALF = 96
PATCH = 16
DEVICES = 128
MESH = pl.DeviceIdType.MESH
HIGHEST = lax.Precision.HIGHEST
EXP_SCALE = 10.0 * math.log2(math.e)
SHIFT = math.exp(5.0)
GROUP = 6
PACE = (0, 0, 0, 8, 8, 30, 20, 0)
GROUP_SCALE = math.exp(-5.0 * GROUP)


def patch_order():
    seen = []
    for x in range(4):
        for y in range(4):
            for z in range(4):
                for k in range(2):
                    for p in ((x, y, z), (y, z, x), (z, x, y)):
                        for q in (p, tuple((-v) % 4 for v in p)):
                            o = q + (k,)
                            if any(o) and o not in seen:
                                seen.append(o)
    return seen


def z_of(zh, zl):
    return zl + zh * (3 - 2 * zl)


def device(x, y, z, k):
    return (x * 4 + z, y * 2 + k)


def unit(rows):
    wide = rows.astype(jnp.float32)
    length = jnp.sqrt(jnp.sum(wide * wide, axis=1, keepdims=True) + EPSILON)
    return (wide / length).astype(jnp.bfloat16)


def dot_t(a, b, precision=None):
    return lax.dot_general(
        a, b, (((1,), (1,)), ((), ())), preferred_element_type=jnp.float32, precision=precision
    )


def dot(a, b, precision=None):
    return lax.dot_general(
        a, b, (((1,), (0,)), ((), ())), preferred_element_type=jnp.float32, precision=precision
    )


def product(parts):
    while len(parts) > 1:
        tail = parts[len(parts) // 2 * 2 :]
        parts = [a * b for a, b in zip(parts[0::2], parts[1::2])] + tail
    return parts[0]


def kernel(
    slot_row,
    pos_row,
    pos_col,
    img_l,
    img_r,
    txt_l,
    txt_r,
    patches,
    learn_out,
    grad_out,
    batches,
    texts,
    images,
    pool,
    slots,
    logit_l,
    logit_r,
    slope,
    grads,
    grad_send,
    grad_recv,
    text_acc,
    image_acc,
    text_send,
    text_recv,
    image_send,
    image_recv,
    pool_sem,
    own_sem,
    text_sems,
    image_sems,
    send_sems,
    recv_sems,
    line_sems,
):
    row = lax.axis_index("row")
    col = lax.axis_index("col")
    x, z = row // 4, row % 4
    y, k = col // 2, col % 2
    zh = z // 2
    zl = (z + zh) % 2
    me = row * 8 + col
    my_text = x * 2 + zl
    my_image = (y * 2 + zh) * 2 + k

    pool_copy = pltpu.make_async_copy(patches, pool.at[pl.ds(0, ROWS)], pool_sem)
    pool_copy.start()

    barrier = pltpu.get_barrier_semaphore()

    lines = [[device((x + d) % 4, y, z, k) for d in (1, 2, 3)]]
    lines.append([device(x, (y + d) % 4, z, k) for d in (1, 2, 3)])
    lines.append([device(x, y, (z + d) % 4, k) for d in (1, 2, 3)])
    lines.append([device(x, y, z, 1 - k)])
    for line in lines:
        for other in line:
            pl.semaphore_signal(barrier, inc=1, device_id=other, device_id_type=MESH)

    places = lax.broadcasted_iota(jnp.int32, (ROWS, ROWS), 0)
    order = (places == pos_row[...]).astype(jnp.float32).astype(jnp.bfloat16)

    def ordered(ref):
        return dot(order, unit(ref[...])).astype(jnp.bfloat16)

    text_learn, text_refer = ordered(txt_l), ordered(txt_r)
    image_learn, image_refer = ordered(img_l), ordered(img_r)
    texts[my_text, 0:2] = text_learn.reshape(2, HALF, D)
    texts[my_text, 2:4] = text_refer.reshape(2, HALF, D)
    images[my_image, 0:2] = image_learn.reshape(2, HALF, D)
    images[my_image, 2:4] = image_refer.reshape(2, HALF, D)

    pl.semaphore_wait(barrier, 10)

    def send(buf, sems, slot, quarter, target, sender):
        part = buf.at[slot, quarter]
        pltpu.make_async_remote_copy(
            src_ref=part,
            dst_ref=part,
            send_sem=send_sems.at[sender],
            recv_sem=sems.at[slot, quarter],
            device_id=target,
            device_id_type=MESH,
        ).start()

    def arrived(buf, sems, slot, quarter):
        part = buf.at[slot, quarter]
        pltpu.make_async_remote_copy(
            src_ref=part,
            dst_ref=part,
            send_sem=send_sems.at[0],
            recv_sem=sems.at[slot, quarter],
            device_id=(row, col),
            device_id_type=MESH,
        ).wait_recv()

    def text_at(dx, dz):
        return ((x + dx) % 4) * 2 + (zl + dz) % 2

    def image_at(dy, dz, dk=0):
        return (((y + dy) % 4) * 2 + (zh + dz) % 2) * 2 + (k + dk) % 2

    z_text, z_image = z_of(zh, 1 - zl), z_of(1 - zh, zl)
    x_next, x_prev, x_pair = (
        device((x + 1) % 4, y, z, k),
        device((x + 3) % 4, y, z, k),
        device(x, y, z_text, k),
    )
    y_next, y_prev, y_pair = (
        device(x, (y + 1) % 4, z, k),
        device(x, (y + 3) % 4, z, k),
        device(x, y, z_image, k),
    )
    sibling = device(x, y, z, 1 - k)

    def send_text(slot, quarter, target):
        send(texts, text_sems, slot, quarter, target, 0)

    def send_image(slot, quarter, target):
        send(images, image_sems, slot, quarter, target, 1)

    def text_here(dx, dz, quarter, *targets):
        arrived(texts, text_sems, text_at(dx, dz), quarter)
        for target in targets:
            send_text(text_at(dx, dz), quarter, target)

    def image_here(dy, dz, quarter, *targets):
        arrived(images, image_sems, image_at(dy, dz), quarter)
        for target in targets:
            send_image(image_at(dy, dz), quarter, target)
        send_image(image_at(dy, dz), quarter, sibling)

    for i in range(4):
        up, down = i, (i + 2) % 4
        send_text(my_text, up, x_next)
        send_image(my_image, up, y_next)
        send_text(my_text, down, x_prev)
        send_image(my_image, down, y_prev)
        send_text(my_text, up, x_pair)
        send_image(my_image, up, y_pair)
        send_image(my_image, up, sibling)

    pool[ROWS] = jnp.zeros((PATCH, D), jnp.bfloat16)
    pool_copy.wait()

    def place(i, carry):
        slots[i] = pool[slot_row[i]]
        return carry

    lax.fori_loop(0, 2 * DEVICES, place, 0)
    own_part = pl.ds(2 * me, 2)
    own_copy = pltpu.make_async_copy(slots.at[own_part], batches.at[own_part], own_sem)
    own_copy.start()

    for i, line in enumerate(lines):
        for other in line:
            pl.semaphore_signal(line_sems.at[i], inc=1, device_id=other, device_id_type=MESH)
        pl.semaphore_wait(line_sems.at[i], len(line))

    waiting = patch_order()

    def send_patches(count):
        for dx, dy, dz, dk in waiting[:count]:
            r = ((x + dx) % 4) * 4 + (z + dz) % 4
            c = ((y + dy) % 4) * 2 + (k + dk) % 2
            pltpu.make_async_remote_copy(
                src_ref=slots.at[pl.ds(2 * (r * 8 + c), 2)],
                dst_ref=batches.at[own_part],
                send_sem=send_sems.at[2],
                recv_sem=recv_sems.at[0],
                device_id=(r, c),
                device_id_type=MESH,
            ).start()
        del waiting[:count]

    send_patches(PACE[0])
    for i in range(2):
        text_here(3, 0, i, x_next)
        image_here(3, 0, i, y_next)
        text_here(1, 0, i + 2, x_prev)
        image_here(1, 0, i + 2, y_prev)
        send_patches(PACE[1])
    for i in range(4):
        text_here(0, 1, i, x_next, x_prev)
        image_here(0, 1, i, y_next, y_prev)
        send_patches(PACE[2])
    for i in range(2):
        text_here(3, 0, i + 2)
        image_here(3, 0, i + 2)
        text_here(1, 0, i)
        image_here(1, 0, i)
    for i in (0, 2, 1, 3):
        text_here(2, 0, i, x_pair)
        image_here(2, 0, i, y_pair)
        send_patches(PACE[3])
    for i in range(4):
        for d in (1, 3, 2):
            text_here(d, 1, i)
            image_here(d, 1, i)
        send_patches(PACE[4])
    for i in range(4):
        for dy in range(4):
            for dz in range(2):
                arrived(images, image_sems, image_at(dy, dz, 1), i)

    text_acc[...] = jnp.zeros_like(text_acc)
    image_acc[...] = jnp.zeros_like(image_acc)

    def pair_tile(step, with_grad):
        text_class = step // 4
        image_class = step // 2 % 2
        image_half = step % 2
        blocks = pl.ds(image_half * 8, 8)
        learn_cols = images[blocks, image_class].reshape(8 * HALF, D)
        logit_l[...] = dot_t(texts[:, text_class].reshape(8 * HALF, D), learn_cols)
        refer_cols = images[blocks, 2 + image_class].reshape(8 * HALF, D)
        logit_r[...] = dot_t(texts[:, 2 + text_class].reshape(8 * HALF, D), refer_cols)

        def one_block(b, total):
            for part in range(2):
                start = pl.multiple_of(b * HALF + part * 48, 16)
                rows = pl.ds(start, 48)
                e_l = jnp.exp2(logit_l[rows, :] * EXP_SCALE)
                e_r = jnp.exp2(logit_r[rows, :] * EXP_SCALE)
                p_l, p_r = e_l + SHIFT, e_r + SHIFT
                if with_grad:
                    slope[rows, :] = (e_l / p_l).astype(jnp.bfloat16)

                def gap(parts_l, parts_r):
                    return jnp.log(product(parts_l) * GROUP_SCALE) - jnp.log(
                        product(parts_r) * GROUP_SCALE
                    )

                across = gap(
                    [p_l[:, 128 * i : 128 * (i + 1)] for i in range(GROUP)],
                    [p_r[:, 128 * i : 128 * (i + 1)] for i in range(GROUP)],
                )
                text_acc[b, text_class, pl.ds(part * 48, 48), :] += across
                total = total + gap(
                    [p_l[8 * i : 8 * (i + 1), :] for i in range(GROUP)],
                    [p_r[8 * i : 8 * (i + 1), :] for i in range(GROUP)],
                )
            return total

        image_acc[image_half, image_class] += lax.fori_loop(
            0, 8, one_block, jnp.zeros((8, 8 * HALF), jnp.float32)
        )
        if with_grad:
            grads[...] += dot(slope[...], learn_cols)

    grads[...] = jnp.zeros_like(grads)

    def with_grad(step, carry):
        pair_tile(step, True)
        return carry

    send_patches(PACE[5])
    lax.fori_loop(0, 2, with_grad, 0)

    def to_text_peers(source, landing, sender, receiver):
        for dx, dz in ((0, 1), (1, 0), (3, 0), (1, 1), (3, 1), (2, 0), (2, 1)):
            slot = text_at(dx, dz)
            pltpu.make_async_remote_copy(
                src_ref=source.at[slot],
                dst_ref=landing.at[my_text],
                send_sem=send_sems.at[sender],
                recv_sem=recv_sems.at[receiver],
                device_id=device(slot // 2, y, z_of(zh, slot % 2), k),
                device_id_type=MESH,
            ).start()

    grad_send[...] = grads[...].reshape(8, HALF, D).astype(jnp.bfloat16)
    to_text_peers(grad_send, grad_recv, 3, 1)

    def without_grad(step, carry):
        pair_tile(step, False)
        return carry

    send_patches(PACE[6])
    lax.fori_loop(2, 5, without_grad, 0)
    send_patches(PACE[7])
    lax.fori_loop(5, 8, without_grad, 0)

    ones = jnp.ones((8, 128), jnp.float32)
    for b in range(8):
        sums = dot_t(ones, text_acc[b].reshape(ROWS, 128), HIGHEST)
        text_send[b, :, 0:ROWS] = sums[0:1]
    to_text_peers(text_send, text_recv, 4, 2)
    for h in range(2):
        for a in range(2):
            image_send[h, :, pl.ds(a * 768, 768)] = jnp.sum(image_acc[h, a], axis=0, keepdims=True)
    for d in range(1, 16):
        slot = (my_image + d) % 16
        pltpu.make_async_remote_copy(
            src_ref=image_send.at[slot // 8],
            dst_ref=image_recv.at[my_image],
            send_sem=send_sems.at[5],
            recv_sem=recv_sems.at[3],
            device_id=device(x, slot // 4, z_of(slot // 2 % 2, zl), slot % 2),
            device_id_type=MESH,
        ).start()
    send_patches(len(waiting))
    text_recv[my_text] = text_send[my_text]
    image_recv[my_image] = image_send[my_image // 8]
    grad_recv[my_text] = grad_send[my_text]

    def all_of(buf, count, sender, receiver):
        part = buf.at[pl.ds(0, count)]
        return pltpu.make_async_remote_copy(
            src_ref=part,
            dst_ref=part,
            send_sem=send_sems.at[sender],
            recv_sem=recv_sems.at[receiver],
            device_id=(row, col),
            device_id_type=MESH,
        )

    own_image = image_learn[0:HALF].astype(jnp.float32)
    cosines = jnp.sum(own_image * text_learn[0:HALF].astype(jnp.float32), axis=1, keepdims=True)
    e = jnp.exp2(cosines * EXP_SCALE)
    as_negative = (e / (e + SHIFT)).astype(jnp.bfloat16).astype(jnp.float32)
    as_positive = -(SHIFT / (e + SHIFT)).astype(jnp.bfloat16).astype(jnp.float32)
    all_of(grad_recv, 7, 3, 1).wait_recv()
    total = (as_positive - as_negative) * own_image
    for b in range(8):
        total = total + grad_recv[b].astype(jnp.float32)
    total = total * 10.0
    own_text = dot(order[0:HALF], txt_l[...])
    length = jnp.sqrt(jnp.sum(own_text * own_text, axis=1, keepdims=True) + EPSILON)
    along = jnp.sum(own_text * total, axis=1, keepdims=True) / (length * length * length)
    result = total / length - own_text * along
    back = (lax.broadcasted_iota(jnp.int32, (ROWS, HALF), 1) == pos_col[...]).astype(jnp.float32)
    grad_out[...] = dot(back, result, HIGHEST)

    diagonal = image_refer.astype(jnp.float32) * text_refer.astype(
        jnp.float32
    ) - image_learn.astype(jnp.float32) * text_learn.astype(jnp.float32)
    score = 20.0 * dot_t(jnp.ones((8, D), jnp.float32), diagonal, HIGHEST)
    all_of(text_recv, 7, 4, 2).wait_recv()
    text_sum = jnp.sum(text_recv[:, :, 0:ROWS], axis=0)
    all_of(image_recv, 15, 5, 3).wait_recv()
    image_sum = jnp.sum(image_recv[...], axis=0)
    wanted = lax.broadcasted_iota(jnp.int32, (768, ROWS), 0)
    place_of = lax.broadcasted_iota(jnp.int32, (768, ROWS), 1)
    base = (my_image % 8) * HALF
    pick_sel = (wanted - base == place_of).astype(jnp.float32)
    pick_uns = ((wanted - base + HALF == place_of) & (place_of >= HALF)).astype(jnp.float32)
    pick_sel = jnp.where(place_of < HALF, pick_sel, 0.0)
    rows8 = lambda v: jnp.broadcast_to(v, (8, v.shape[1]))
    score = score + rows8(text_sum)
    score = score + dot(rows8(image_sum[:, 0:768]), pick_sel, HIGHEST)
    score = score + dot(rows8(image_sum[:, 768:1536]), pick_uns, HIGHEST)
    learn_out[...] = dot(score, order.astype(jnp.float32), HIGHEST)[0:1]

    all_of(slots, 2 * (DEVICES - 1), 2, 0).wait_send()
    own_copy.wait()
    all_of(texts, 7, 0, 0).wait_send()
    all_of(images, 15, 1, 0).wait_send()
    all_of(grad_send, 7, 3, 1).wait_send()
    all_of(text_send, 7, 4, 2).wait_send()
    all_of(image_recv, 15, 5, 3).wait_send()
    all_of(batches, 2 * (DEVICES - 1), 2, 0).wait_recv()


def on_device(img_learner, img_refer, txt_learner, txt_refer, patches, chosen, trainer_of):
    flat = lax.axis_index("row") * lax.axis_size("col") + lax.axis_index("col")
    offsets = chosen - flat * ROWS
    rows = jnp.arange(ROWS, dtype=jnp.int32)
    entries = jnp.arange(HALF, dtype=jnp.int32)
    hits = offsets[:, None] == rows[None, :]
    selected = jnp.any(hits, axis=0)
    as_selected = jnp.sum(jnp.where(hits, entries[:, None], 0), axis=0)
    before = jnp.sum(((rows[:, None] < rows[None, :]) & ~selected[:, None]).astype(jnp.int32), axis=0)
    position = jnp.where(selected, as_selected, HALF + before).astype(jnp.int32)
    owners = trainer_of[:, 0]
    earlier = (owners[:, None] == owners[None, :]) & (entries[None, :] < entries[:, None])
    targets = 2 * owners + jnp.sum(earlier.astype(jnp.int32), axis=1)
    wanted = targets[:, None] == jnp.arange(2 * DEVICES, dtype=jnp.int32)[None, :]
    slot_row = ROWS + jnp.sum(jnp.where(wanted, offsets[:, None] - ROWS, 0), axis=0)

    vmem = pl.BlockSpec(memory_space=pltpu.VMEM)
    anywhere = pl.BlockSpec(memory_space=pl.ANY)
    bf16, f32 = jnp.bfloat16, jnp.float32
    learnability, text_grad, batches = pl.pallas_call(
        kernel,
        out_shape=(
            jax.ShapeDtypeStruct((1, ROWS), f32),
            jax.ShapeDtypeStruct((ROWS, D), f32),
            jax.ShapeDtypeStruct((2 * DEVICES, PATCH, D), bf16),
        ),
        in_specs=[pl.BlockSpec(memory_space=pltpu.SMEM)] + [vmem] * 6 + [anywhere],
        out_specs=(vmem, vmem, anywhere),
        scratch_shapes=[
            pltpu.VMEM((8, 4, HALF, D), bf16),
            pltpu.VMEM((16, 4, HALF, D), bf16),
            pltpu.VMEM((ROWS + 1, PATCH, D), bf16),
            pltpu.VMEM((2 * DEVICES, PATCH, D), bf16),
            pltpu.VMEM((8 * HALF, 8 * HALF), f32),
            pltpu.VMEM((8 * HALF, 8 * HALF), f32),
            pltpu.VMEM((8 * HALF, 8 * HALF), bf16),
            pltpu.VMEM((8 * HALF, D), f32),
            pltpu.VMEM((8, HALF, D), bf16),
            pltpu.VMEM((8, HALF, D), bf16),
            pltpu.VMEM((8, 2, HALF, 128), f32),
            pltpu.VMEM((2, 2, 8, 8 * HALF), f32),
            pltpu.VMEM((8, 1, 256), f32),
            pltpu.VMEM((8, 1, 256), f32),
            pltpu.VMEM((2, 1, 1536), f32),
            pltpu.VMEM((16, 1, 1536), f32),
            pltpu.SemaphoreType.DMA,
            pltpu.SemaphoreType.DMA,
            pltpu.SemaphoreType.DMA((8, 4)),
            pltpu.SemaphoreType.DMA((16, 4)),
            pltpu.SemaphoreType.DMA((6,)),
            pltpu.SemaphoreType.DMA((4,)),
            pltpu.SemaphoreType.REGULAR((4,)),
        ],
        compiler_params=pltpu.CompilerParams(
            collective_id=0, has_side_effects=True, vmem_limit_bytes=60 * 1024 * 1024
        ),
        name="jest",
    )(
        slot_row,
        position[None, :],
        position[:, None],
        img_learner,
        img_refer,
        txt_learner,
        txt_refer,
        patches,
    )
    return (learnability[0], text_grad, batches)


def solution(mesh):
    placed = (
        P(("row", "col"), None),
        P(("row", "col"), None),
        P(("row", "col"), None),
        P(("row", "col"), None),
        P(("row", "col"), None, None),
        P(("row", "col")),
        P(("row", "col"), None),
    )
    return jax.shard_map(
        on_device,
        mesh=mesh,
        in_specs=placed,
        out_specs=(P(("row", "col")), P(("row", "col"), None), P(("row", "col"), None, None)),
        check_vma=False,
    )
```

```python
import math
import jax
import jax.numpy as jnp
from jax import lax
from jax.experimental import pallas as pl
from jax.experimental.pallas import tpu as pltpu
from jax.sharding import PartitionSpec as P

EPSILON = 1e-06
D = 768
ROWS = 192
HALF = 96
PATCH = 16
DEVICES = 128
MESH = pl.DeviceIdType.MESH
HIGHEST = lax.Precision.HIGHEST
EXP_SCALE = 10.0 * math.log2(math.e)
SHIFT = math.exp(5.0)
GROUP = 6
PACE = (0, 0, 0, 8, 8, 30, 20, 0)
GROUP_SCALE = math.exp(-5.0 * GROUP)


def patch_order():
    seen = []
    for x in range(4):
        for y in range(4):
            for z in range(4):
                for k in range(2):
                    for p in ((x, y, z), (y, z, x), (z, x, y)):
                        for q in (p, tuple((-v) % 4 for v in p)):
                            o = q + (k,)
                            if any(o) and o not in seen:
                                seen.append(o)
    return sorted(seen, key=lambda o: o[3])


def z_of(zh, zl):
    return zl + zh * (3 - 2 * zl)


def device(x, y, z, k):
    return (x * 4 + z, y * 2 + k)


def unit(rows):
    wide = rows.astype(jnp.float32)
    length = jnp.sqrt(jnp.sum(wide * wide, axis=1, keepdims=True) + EPSILON)
    return (wide / length).astype(jnp.bfloat16)


def dot_t(a, b, precision=None):
    return lax.dot_general(
        a, b, (((1,), (1,)), ((), ())), preferred_element_type=jnp.float32, precision=precision
    )


def dot(a, b, precision=None):
    return lax.dot_general(
        a, b, (((1,), (0,)), ((), ())), preferred_element_type=jnp.float32, precision=precision
    )


def product(parts):
    while len(parts) > 1:
        tail = parts[len(parts) // 2 * 2 :]
        parts = [a * b for a, b in zip(parts[0::2], parts[1::2])] + tail
    return parts[0]


def kernel(
    slot_row,
    marks,
    pos_row,
    pos_col,
    img_l,
    img_r,
    txt_l,
    txt_r,
    patches,
    learn_out,
    grad_out,
    batches,
    summary,
    texts,
    images,
    pool,
    slots,
    logit_l,
    logit_r,
    slope,
    grads,
    grad_send,
    grad_recv,
    text_acc,
    image_acc,
    text_send,
    text_recv,
    image_send,
    image_recv,
    pool_sem,
    own_sem,
    text_sems,
    image_sems,
    send_sems,
    recv_sems,
    line_sems,
    flags,
    flag_sems,
):
    row = lax.axis_index("row")
    col = lax.axis_index("col")
    x, z = row // 4, row % 4
    y, k = col // 2, col % 2
    zh = z // 2
    zl = (z + zh) % 2
    me = row * 8 + col
    my_text = x * 2 + zl
    my_image = (y * 2 + zh) * 2 + k

    pool_copy = pltpu.make_async_copy(patches, pool.at[pl.ds(0, ROWS)], pool_sem)
    pool_copy.start()

    barrier = pltpu.get_barrier_semaphore()

    lines = [[device((x + d) % 4, y, z, k) for d in (1, 2, 3)]]
    lines.append([device(x, (y + d) % 4, z, k) for d in (1, 2, 3)])
    lines.append([device(x, y, (z + d) % 4, k) for d in (1, 2, 3)])
    lines.append([device(x, y, z, 1 - k)])
    for line in lines:
        for other in line:
            pl.semaphore_signal(barrier, inc=1, device_id=other, device_id_type=MESH)

    places = lax.broadcasted_iota(jnp.int32, (ROWS, ROWS), 0)
    order = (places == pos_row[...]).astype(jnp.float32).astype(jnp.bfloat16)

    def ordered(ref):
        return dot(order, unit(ref[...])).astype(jnp.bfloat16)

    text_learn, text_refer = ordered(txt_l), ordered(txt_r)
    image_learn, image_refer = ordered(img_l), ordered(img_r)
    texts[my_text, 0:2] = text_learn.reshape(2, HALF, D)
    texts[my_text, 2:4] = text_refer.reshape(2, HALF, D)
    images[my_image, 0:2] = image_learn.reshape(2, HALF, D)
    images[my_image, 2:4] = image_refer.reshape(2, HALF, D)

    pl.semaphore_wait(barrier, 10)

    flags[k * 64 + z * 16 + y * 4 + x] = marks[...]
    flag_parts = [
        flags.at[pl.ds(k * 64 + z * 16 + y * 4 + x, 1)],
        flags.at[pl.ds(k * 64 + z * 16 + y * 4, 4)],
        flags.at[pl.ds(k * 64 + z * 16, 16)],
        flags.at[pl.ds(k * 64, 64)],
    ]

    def send_flags(i):
        for other in lines[i]:
            pltpu.make_async_remote_copy(
                src_ref=flag_parts[i],
                dst_ref=flag_parts[i],
                send_sem=send_sems.at[6],
                recv_sem=flag_sems.at[i],
                device_id=other,
                device_id_type=MESH,
            ).start()

    def flags_here(i):
        part = flags.at[pl.ds(0, (3, 12, 48, 64)[i])]
        pltpu.make_async_remote_copy(
            src_ref=part,
            dst_ref=part,
            send_sem=send_sems.at[6],
            recv_sem=flag_sems.at[i],
            device_id=(row, col),
            device_id_type=MESH,
        ).wait_recv()

    send_flags(0)

    def send(buf, sems, slot, quarter, target, sender):
        part = buf.at[slot, quarter]
        pltpu.make_async_remote_copy(
            src_ref=part,
            dst_ref=part,
            send_sem=send_sems.at[sender],
            recv_sem=sems.at[slot, quarter],
            device_id=target,
            device_id_type=MESH,
        ).start()

    def arrived(buf, sems, slot, quarter):
        part = buf.at[slot, quarter]
        pltpu.make_async_remote_copy(
            src_ref=part,
            dst_ref=part,
            send_sem=send_sems.at[0],
            recv_sem=sems.at[slot, quarter],
            device_id=(row, col),
            device_id_type=MESH,
        ).wait_recv()

    def text_at(dx, dz):
        return ((x + dx) % 4) * 2 + (zl + dz) % 2

    def image_at(dy, dz, dk=0):
        return (((y + dy) % 4) * 2 + (zh + dz) % 2) * 2 + (k + dk) % 2

    z_text, z_image = z_of(zh, 1 - zl), z_of(1 - zh, zl)
    x_next, x_prev, x_pair = (
        device((x + 1) % 4, y, z, k),
        device((x + 3) % 4, y, z, k),
        device(x, y, z_text, k),
    )
    y_next, y_prev, y_pair = (
        device(x, (y + 1) % 4, z, k),
        device(x, (y + 3) % 4, z, k),
        device(x, y, z_image, k),
    )
    sibling = device(x, y, z, 1 - k)

    def send_text(slot, quarter, target):
        send(texts, text_sems, slot, quarter, target, 0)

    def send_image(slot, quarter, target):
        send(images, image_sems, slot, quarter, target, 1)

    def text_here(dx, dz, quarter, *targets):
        arrived(texts, text_sems, text_at(dx, dz), quarter)
        for target in targets:
            send_text(text_at(dx, dz), quarter, target)

    def image_here(dy, dz, quarter, *targets):
        arrived(images, image_sems, image_at(dy, dz), quarter)
        for target in targets:
            send_image(image_at(dy, dz), quarter, target)
        send_image(image_at(dy, dz), quarter, sibling)

    for i in range(4):
        up, down = i, (i + 2) % 4
        send_text(my_text, up, x_next)
        send_image(my_image, up, y_next)
        send_text(my_text, down, x_prev)
        send_image(my_image, down, y_prev)
        send_text(my_text, up, x_pair)
        send_image(my_image, up, y_pair)
        send_image(my_image, up, sibling)

    pool[ROWS] = jnp.zeros((PATCH, D), jnp.bfloat16)
    pool_copy.wait()

    def place(i, carry):
        slots[i] = pool[slot_row[i]]
        return carry

    lax.fori_loop(0, 2 * DEVICES, place, 0)
    own_copy = pltpu.make_async_copy(
        slots.at[pl.ds(2 * me, 2)], batches.at[row * 4 + y, pl.ds(2 * k, 2)], own_sem
    )
    own_copy.start()

    for i, line in enumerate(lines):
        for other in line:
            pl.semaphore_signal(line_sems.at[i], inc=1, device_id=other, device_id_type=MESH)
        pl.semaphore_wait(line_sems.at[i], len(line))

    waiting = patch_order()

    def send_patches(count):
        for dx, dy, dz, dk in waiting[:count]:
            r = ((x + dx) % 4) * 4 + (z + dz) % 4
            c = ((y + dy) % 4) * 2 + (k + dk) % 2
            count_here = 2 - dk
            pltpu.make_async_remote_copy(
                src_ref=slots.at[pl.ds(2 * (r * 8 + c), count_here)],
                dst_ref=batches.at[row * 4 + y, pl.ds(2 * k, count_here)],
                send_sem=send_sems.at[2],
                recv_sem=recv_sems.at[4 * dk],
                device_id=(r, c),
                device_id_type=MESH,
            ).start()
        del waiting[:count]

    flags_here(0)
    send_flags(1)
    send_patches(PACE[0])
    for i in range(2):
        text_here(3, 0, i, x_next)
        image_here(3, 0, i, y_next)
        text_here(1, 0, i + 2, x_prev)
        image_here(1, 0, i + 2, y_prev)
        send_patches(PACE[1])
    for i in range(4):
        text_here(0, 1, i, x_next, x_prev)
        image_here(0, 1, i, y_next, y_prev)
        send_patches(PACE[2])
    for i in range(2):
        text_here(3, 0, i + 2)
        image_here(3, 0, i + 2)
        text_here(1, 0, i)
        image_here(1, 0, i)
    flags_here(1)
    send_flags(2)
    for i in (0, 2, 1, 3):
        text_here(2, 0, i, x_pair)
        image_here(2, 0, i, y_pair)
        send_patches(PACE[3])
    for i in range(4):
        for d in (1, 3, 2):
            text_here(d, 1, i)
            image_here(d, 1, i)
        send_patches(PACE[4])
    for i in range(4):
        for dy in range(4):
            for dz in range(2):
                arrived(images, image_sems, image_at(dy, dz, 1), i)

    flags_here(2)
    send_flags(3)
    text_acc[...] = jnp.zeros_like(text_acc)
    image_acc[...] = jnp.zeros_like(image_acc)

    def pair_tile(step, with_grad):
        text_class = step // 4
        image_class = step // 2 % 2
        image_half = step % 2
        blocks = pl.ds(image_half * 8, 8)
        learn_cols = images[blocks, image_class].reshape(8 * HALF, D)
        logit_l[...] = dot_t(texts[:, text_class].reshape(8 * HALF, D), learn_cols)
        refer_cols = images[blocks, 2 + image_class].reshape(8 * HALF, D)
        logit_r[...] = dot_t(texts[:, 2 + text_class].reshape(8 * HALF, D), refer_cols)

        def one_block(b, total):
            for part in range(2):
                start = pl.multiple_of(b * HALF + part * 48, 16)
                rows = pl.ds(start, 48)
                e_l = jnp.exp2(logit_l[rows, :] * EXP_SCALE)
                e_r = jnp.exp2(logit_r[rows, :] * EXP_SCALE)
                p_l, p_r = e_l + SHIFT, e_r + SHIFT
                if with_grad:
                    slope[rows, :] = (e_l / p_l).astype(jnp.bfloat16)

                def gap(parts_l, parts_r):
                    return jnp.log(product(parts_l) * GROUP_SCALE) - jnp.log(
                        product(parts_r) * GROUP_SCALE
                    )

                across = gap(
                    [p_l[:, 128 * i : 128 * (i + 1)] for i in range(GROUP)],
                    [p_r[:, 128 * i : 128 * (i + 1)] for i in range(GROUP)],
                )
                text_acc[b, text_class, pl.ds(part * 48, 48), :] += across
                total = total + gap(
                    [p_l[8 * i : 8 * (i + 1), :] for i in range(GROUP)],
                    [p_r[8 * i : 8 * (i + 1), :] for i in range(GROUP)],
                )
            return total

        image_acc[image_half, image_class] += lax.fori_loop(
            0, 8, one_block, jnp.zeros((8, 8 * HALF), jnp.float32)
        )
        if with_grad:
            grads[...] += dot(slope[...], learn_cols)

    grads[...] = jnp.zeros_like(grads)

    def with_grad(step, carry):
        pair_tile(step, True)
        return carry

    send_patches(PACE[5])
    lax.fori_loop(0, 2, with_grad, 0)

    def to_text_peers(source, landing, sender, receiver):
        for dx, dz in ((0, 1), (1, 0), (3, 0), (1, 1), (3, 1), (2, 0), (2, 1)):
            slot = text_at(dx, dz)
            pltpu.make_async_remote_copy(
                src_ref=source.at[slot],
                dst_ref=landing.at[my_text],
                send_sem=send_sems.at[sender],
                recv_sem=recv_sems.at[receiver],
                device_id=device(slot // 2, y, z_of(zh, slot % 2), k),
                device_id_type=MESH,
            ).start()

    grad_send[...] = grads[...].reshape(8, HALF, D).astype(jnp.bfloat16)
    to_text_peers(grad_send, grad_recv, 3, 1)

    def without_grad(step, carry):
        pair_tile(step, False)
        return carry

    send_patches(PACE[6])
    lax.fori_loop(2, 5, without_grad, 0)
    send_patches(PACE[7])
    lax.fori_loop(5, 8, without_grad, 0)

    ones = jnp.ones((8, 128), jnp.float32)
    for b in range(8):
        sums = dot_t(ones, text_acc[b].reshape(ROWS, 128), HIGHEST)
        text_send[b, :, 0:ROWS] = sums[0:1]
    to_text_peers(text_send, text_recv, 4, 2)
    for h in range(2):
        for a in range(2):
            image_send[h, :, pl.ds(a * 768, 768)] = jnp.sum(image_acc[h, a], axis=0, keepdims=True)
    for d in range(1, 16):
        slot = (my_image + d) % 16
        pltpu.make_async_remote_copy(
            src_ref=image_send.at[slot // 8],
            dst_ref=image_recv.at[my_image],
            send_sem=send_sems.at[5],
            recv_sem=recv_sems.at[3],
            device_id=device(x, slot // 4, z_of(slot // 2 % 2, zl), slot % 2),
            device_id_type=MESH,
        ).start()
    send_patches(len(waiting))
    text_recv[my_text] = text_send[my_text]
    image_recv[my_image] = image_send[my_image // 8]
    grad_recv[my_text] = grad_send[my_text]

    def all_of(buf, count, sender, receiver):
        part = buf.at[pl.ds(0, count)]
        return pltpu.make_async_remote_copy(
            src_ref=part,
            dst_ref=part,
            send_sem=send_sems.at[sender],
            recv_sem=recv_sems.at[receiver],
            device_id=(row, col),
            device_id_type=MESH,
        )

    own_image = image_learn[0:HALF].astype(jnp.float32)
    cosines = jnp.sum(own_image * text_learn[0:HALF].astype(jnp.float32), axis=1, keepdims=True)
    e = jnp.exp2(cosines * EXP_SCALE)
    as_negative = (e / (e + SHIFT)).astype(jnp.bfloat16).astype(jnp.float32)
    as_positive = -(SHIFT / (e + SHIFT)).astype(jnp.bfloat16).astype(jnp.float32)
    all_of(grad_recv, 7, 3, 1).wait_recv()
    total = (as_positive - as_negative) * own_image
    for b in range(8):
        total = total + grad_recv[b].astype(jnp.float32)
    total = total * 10.0
    own_text = dot(order[0:HALF], txt_l[...])
    length = jnp.sqrt(jnp.sum(own_text * own_text, axis=1, keepdims=True) + EPSILON)
    along = jnp.sum(own_text * total, axis=1, keepdims=True) / (length * length * length)
    result = total / length - own_text * along
    back = (lax.broadcasted_iota(jnp.int32, (ROWS, HALF), 1) == pos_col[...]).astype(jnp.float32)
    grad_out[...] = dot(back, result, HIGHEST)

    diagonal = image_refer.astype(jnp.float32) * text_refer.astype(
        jnp.float32
    ) - image_learn.astype(jnp.float32) * text_learn.astype(jnp.float32)
    score = 20.0 * dot_t(jnp.ones((8, D), jnp.float32), diagonal, HIGHEST)
    all_of(text_recv, 7, 4, 2).wait_recv()
    text_sum = jnp.sum(text_recv[:, :, 0:ROWS], axis=0)
    all_of(image_recv, 15, 5, 3).wait_recv()
    image_sum = jnp.sum(image_recv[...], axis=0)
    wanted = lax.broadcasted_iota(jnp.int32, (768, ROWS), 0)
    place_of = lax.broadcasted_iota(jnp.int32, (768, ROWS), 1)
    base = (my_image % 8) * HALF
    pick_sel = (wanted - base == place_of).astype(jnp.float32)
    pick_uns = ((wanted - base + HALF == place_of) & (place_of >= HALF)).astype(jnp.float32)
    pick_sel = jnp.where(place_of < HALF, pick_sel, 0.0)
    rows8 = lambda v: jnp.broadcast_to(v, (8, v.shape[1]))
    score = score + rows8(text_sum)
    score = score + dot(rows8(image_sum[:, 0:768]), pick_sel, HIGHEST)
    score = score + dot(rows8(image_sum[:, 768:1536]), pick_uns, HIGHEST)
    learn_out[...] = dot(score, order.astype(jnp.float32), HIGHEST)[0:1]

    flags_here(3)
    second = flags[...].reshape(DEVICES, DEVICES)
    names = lax.broadcasted_iota(jnp.int32, (8, DEVICES), 1)
    own_column = (names == me).astype(jnp.float32)
    other_column = (names == me + 1 - 2 * k).astype(jnp.float32)
    source = lax.broadcasted_iota(jnp.int32, (DEVICES, DEVICES), 0)
    target = lax.broadcasted_iota(jnp.int32, (DEVICES, DEVICES), 1)
    by_line = (target % 2) * 64 + (target // 8 % 4) * 16 + (target // 2 % 4) * 4 + target // 32
    sorted_out = (source == by_line).astype(jnp.float32)
    mine = dot(dot_t(own_column, second), sorted_out)
    others = dot(dot_t(other_column, second), sorted_out)
    crowded = mine * others * k.astype(jnp.float32)
    summary[0] = mine - crowded
    summary[1] = crowded
    next_one = ((source == target + 1) & (target % 2 == 0)).astype(jnp.float32)
    doubles = jnp.sum(second * dot(second, next_one), axis=0, keepdims=True)
    summary[2] = jnp.broadcast_to(jnp.sum(doubles, axis=1, keepdims=True), (8, DEVICES))

    def rows_of(count, sender, receiver):
        part = slots.at[pl.ds(0, count)]
        return pltpu.make_async_remote_copy(
            src_ref=part,
            dst_ref=part,
            send_sem=send_sems.at[sender],
            recv_sem=recv_sems.at[receiver],
            device_id=(row, col),
            device_id_type=MESH,
        )

    own_copy.wait()
    rows_of(126, 2, 0).wait_recv()
    exchange = pltpu.make_async_remote_copy(
        src_ref=batches.at[:, 2 * k + 1],
        dst_ref=batches.at[:, 2 * k + 1],
        send_sem=send_sems.at[7],
        recv_sem=recv_sems.at[5],
        device_id=sibling,
        device_id_type=MESH,
    )
    exchange.start()
    rows_of(64, 2, 4).wait_recv()
    exchange.wait_send()
    rows_of(64, 2, 5).wait_recv()

    rows_of(190, 2, 0).wait_send()
    all_of(flags, 127, 6, 0).wait_send()
    all_of(texts, 7, 0, 0).wait_send()
    all_of(images, 15, 1, 0).wait_send()
    all_of(grad_send, 7, 3, 1).wait_send()
    all_of(text_send, 7, 4, 2).wait_send()
    all_of(image_recv, 15, 5, 3).wait_send()


def left_over_kernel(slot_row, patches, landing, pool, slots, sems, line_sems):
    row = lax.axis_index("row")
    col = lax.axis_index("col")
    x, z = row // 4, row % 4
    y, k = col // 2, col % 2
    me = row * 8 + col
    pool_copy = pltpu.make_async_copy(patches, pool.at[pl.ds(0, ROWS)], sems.at[0])
    pool_copy.start()
    barrier = pltpu.get_barrier_semaphore()
    lines = [[device((x + d) % 4, y, z, k) for d in (1, 2, 3)]]
    lines.append([device(x, (y + d) % 4, z, k) for d in (1, 2, 3)])
    lines.append([device(x, y, (z + d) % 4, k) for d in (1, 2, 3)])
    lines.append([device(x, y, z, 1 - k)])
    for line in lines:
        for other in line:
            pl.semaphore_signal(barrier, inc=1, device_id=other, device_id_type=MESH)
    pl.semaphore_wait(barrier, 10)
    for i, line in enumerate(lines):
        for other in line:
            pl.semaphore_signal(line_sems.at[i], inc=1, device_id=other, device_id_type=MESH)
        pl.semaphore_wait(line_sems.at[i], len(line))
    pool[ROWS] = jnp.zeros((PATCH, D), jnp.bfloat16)
    pool_copy.wait()

    def place(i, carry):
        slots[i] = pool[slot_row[i]]
        return carry

    lax.fori_loop(0, DEVICES // 2, place, 0)

    def to_chip(source, target):
        return pltpu.make_async_remote_copy(
            src_ref=slots.at[source],
            dst_ref=landing.at[me],
            send_sem=sems.at[1],
            recv_sem=sems.at[2],
            device_id=target,
            device_id_type=MESH,
        )

    for dx, dy, dz, dk in patch_order()[:63]:
        r, c = ((x + dx) % 4) * 4 + (z + dz) % 4, (y + dy) % 4
        to_chip(r * 4 + c, (r, c * 2 + 1)).start()

    def total(count):
        part = pool.at[pl.ds(0, count)]
        return pltpu.make_async_remote_copy(
            src_ref=part,
            dst_ref=part,
            send_sem=sems.at[1],
            recv_sem=sems.at[2],
            device_id=(row, col),
            device_id_type=MESH,
        )

    @pl.when(k == 0)
    def _():
        to_chip(row * 4 + y, (row, y * 2 + 1)).start()
        total(64).wait_send()

    @pl.when(k == 1)
    def _():
        own = pltpu.make_async_copy(slots.at[row * 4 + y], landing.at[me], sems.at[3])
        own.start()
        total(127).wait_recv()
        own.wait()
        total(63).wait_send()


def on_device(img_learner, img_refer, txt_learner, txt_refer, patches, chosen, trainer_of):
    flat = lax.axis_index("row") * lax.axis_size("col") + lax.axis_index("col")
    offsets = chosen - flat * ROWS
    rows = jnp.arange(ROWS, dtype=jnp.int32)
    entries = jnp.arange(HALF, dtype=jnp.int32)
    hits = offsets[:, None] == rows[None, :]
    selected = jnp.any(hits, axis=0)
    as_selected = jnp.sum(jnp.where(hits, entries[:, None], 0), axis=0)
    before = jnp.sum(((rows[:, None] < rows[None, :]) & ~selected[:, None]).astype(jnp.int32), axis=0)
    position = jnp.where(selected, as_selected, HALF + before).astype(jnp.int32)
    owners = trainer_of[:, 0]
    earlier = (owners[:, None] == owners[None, :]) & (entries[None, :] < entries[:, None])
    targets = 2 * owners + jnp.sum(earlier.astype(jnp.int32), axis=1)
    wanted = targets[:, None] == jnp.arange(2 * DEVICES, dtype=jnp.int32)[None, :]
    slot_row = ROWS + jnp.sum(jnp.where(wanted, offsets[:, None] - ROWS, 0), axis=0)

    slot_row = slot_row.reshape(DEVICES, 2)
    seconds = slot_row[:, 1]
    pairs = seconds.reshape(DEVICES // 2, 2)
    carried = jnp.where(pairs[:, 0] < ROWS, pairs[:, 0], pairs[:, 1])
    left_over = jnp.where(pairs[:, 0] < ROWS, pairs[:, 1], ROWS)
    plan = jnp.stack([slot_row[:, 0], jnp.repeat(carried, 2)], axis=1)

    vmem = pl.BlockSpec(memory_space=pltpu.VMEM)
    anywhere = pl.BlockSpec(memory_space=pl.ANY)
    bf16, f32 = jnp.bfloat16, jnp.float32
    learnability, text_grad, batches, summary = pl.pallas_call(
        kernel,
        out_shape=(
            jax.ShapeDtypeStruct((1, ROWS), f32),
            jax.ShapeDtypeStruct((ROWS, D), f32),
            jax.ShapeDtypeStruct((DEVICES // 2, 4, PATCH, D), bf16),
            jax.ShapeDtypeStruct((3, 8, DEVICES), f32),
        ),
        in_specs=[pl.BlockSpec(memory_space=pltpu.SMEM)] + [vmem] * 7 + [anywhere],
        out_specs=(vmem, vmem, anywhere, vmem),
        scratch_shapes=[
            pltpu.VMEM((8, 4, HALF, D), bf16),
            pltpu.VMEM((16, 4, HALF, D), bf16),
            pltpu.VMEM((ROWS + 1, PATCH, D), bf16),
            pltpu.VMEM((2 * DEVICES, PATCH, D), bf16),
            pltpu.VMEM((8 * HALF, 8 * HALF), f32),
            pltpu.VMEM((8 * HALF, 8 * HALF), f32),
            pltpu.VMEM((8 * HALF, 8 * HALF), bf16),
            pltpu.VMEM((8 * HALF, D), f32),
            pltpu.VMEM((8, HALF, D), bf16),
            pltpu.VMEM((8, HALF, D), bf16),
            pltpu.VMEM((8, 2, HALF, 128), f32),
            pltpu.VMEM((2, 2, 8, 8 * HALF), f32),
            pltpu.VMEM((8, 1, 256), f32),
            pltpu.VMEM((8, 1, 256), f32),
            pltpu.VMEM((2, 1, 1536), f32),
            pltpu.VMEM((16, 1, 1536), f32),
            pltpu.SemaphoreType.DMA,
            pltpu.SemaphoreType.DMA,
            pltpu.SemaphoreType.DMA((8, 4)),
            pltpu.SemaphoreType.DMA((16, 4)),
            pltpu.SemaphoreType.DMA((8,)),
            pltpu.SemaphoreType.DMA((6,)),
            pltpu.SemaphoreType.REGULAR((4,)),
            pltpu.VMEM((DEVICES, 1, DEVICES), f32),
            pltpu.SemaphoreType.DMA((4,)),
        ],
        compiler_params=pltpu.CompilerParams(
            collective_id=0, has_side_effects=True, vmem_limit_bytes=60 * 1024 * 1024
        ),
        name="jest",
    )(
        plan.reshape(2 * DEVICES),
        (seconds < ROWS).astype(f32)[None, :],
        position[None, :],
        position[:, None],
        img_learner,
        img_refer,
        txt_learner,
        txt_refer,
        patches,
    )
    batches = batches.reshape(DEVICES, 2, PATCH, D)
    carried_here, crowded_here = summary[0, 0] > 0, summary[1, 0] > 0
    keep = jnp.stack([jnp.ones_like(carried_here), carried_here], axis=1)[:, :, None, None]
    is_second = jnp.array([False, True])[None, :, None, None]

    def with_left_over():
        extra = pl.pallas_call(
            left_over_kernel,
            out_shape=jax.ShapeDtypeStruct((DEVICES, PATCH, D), bf16),
            in_specs=[pl.BlockSpec(memory_space=pltpu.SMEM), anywhere],
            out_specs=anywhere,
            scratch_shapes=[
                pltpu.VMEM((ROWS + 1, PATCH, D), bf16),
                pltpu.VMEM((DEVICES // 2, PATCH, D), bf16),
                pltpu.SemaphoreType.DMA((4,)),
                pltpu.SemaphoreType.REGULAR((4,)),
            ],
            compiler_params=pltpu.CompilerParams(
                collective_id=1, has_side_effects=True, vmem_limit_bytes=32 * 1024 * 1024
            ),
            name="left_over",
        )(left_over, patches)
        base = jnp.where(keep, batches, 0)
        take = crowded_here[:, None, None, None] & is_second
        return jnp.where(take, extra[:, None], base).reshape(2 * DEVICES, PATCH, D)

    def without_left_over():
        return jnp.where(keep, batches, 0).reshape(2 * DEVICES, PATCH, D)

    routed = lax.cond(summary[2, 0, 0] > 0, with_left_over, without_left_over)
    return (learnability[0], text_grad, routed)


def solution(mesh):
    placed = (
        P(("row", "col"), None),
        P(("row", "col"), None),
        P(("row", "col"), None),
        P(("row", "col"), None),
        P(("row", "col"), None, None),
        P(("row", "col")),
        P(("row", "col"), None),
    )
    return jax.shard_map(
        on_device,
        mesh=mesh,
        in_specs=placed,
        out_specs=(P(("row", "col")), P(("row", "col"), None), P(("row", "col"), None, None)),
        check_vma=False,
    )
```

```python
import math
import jax
import jax.numpy as jnp
from jax import lax
from jax.experimental import pallas as pl
from jax.experimental.pallas import tpu as pltpu
from jax.sharding import PartitionSpec as P

EPSILON = 1e-06
D = 768
ROWS = 192
HALF = 96
PATCH = 16
DEVICES = 128
MESH = pl.DeviceIdType.MESH
HIGHEST = lax.Precision.HIGHEST
EXP_SCALE = 10.0 * math.log2(math.e)
SHIFT = math.exp(5.0)
GROUP = 6
PACE = (0, 0, 0, 8, 8, 30, 20, 0)
GROUP_SCALE = math.exp(-5.0 * GROUP)


def patch_order():
    seen = []
    for x in range(4):
        for y in range(4):
            for z in range(4):
                for k in range(2):
                    for p in ((x, y, z), (y, z, x), (z, x, y)):
                        for q in (p, tuple((-v) % 4 for v in p)):
                            o = q + (k,)
                            if any(o) and o not in seen:
                                seen.append(o)
    return sorted(seen, key=lambda o: o[3])


def z_of(zh, zl):
    return zl + zh * (3 - 2 * zl)


def device(x, y, z, k):
    return (x * 4 + z, y * 2 + k)


def unit(rows):
    wide = rows.astype(jnp.float32)
    length = jnp.sqrt(jnp.sum(wide * wide, axis=1, keepdims=True) + EPSILON)
    return (wide / length).astype(jnp.bfloat16)


def dot_t(a, b, precision=None):
    return lax.dot_general(
        a, b, (((1,), (1,)), ((), ())), preferred_element_type=jnp.float32, precision=precision
    )


def dot(a, b, precision=None):
    return lax.dot_general(
        a, b, (((1,), (0,)), ((), ())), preferred_element_type=jnp.float32, precision=precision
    )


def product(parts):
    while len(parts) > 1:
        tail = parts[len(parts) // 2 * 2 :]
        parts = [a * b for a, b in zip(parts[0::2], parts[1::2])] + tail
    return parts[0]


def kernel(
    slot_row,
    marks,
    pos_row,
    img_l,
    img_r,
    txt_l,
    txt_r,
    patches,
    learn_out,
    grad_out,
    batches,
    summary,
    texts,
    images,
    pool,
    slots,
    logit_l,
    logit_r,
    slope,
    grads,
    grad_send,
    grad_recv,
    text_acc,
    image_acc,
    text_send,
    text_recv,
    image_send,
    image_recv,
    pool_sem,
    own_sem,
    text_sems,
    image_sems,
    send_sems,
    recv_sems,
    line_sems,
    flags,
    flag_sems,
):
    row = lax.axis_index("row")
    col = lax.axis_index("col")
    x, z = row // 4, row % 4
    y, k = col // 2, col % 2
    zh = z // 2
    zl = (z + zh) % 2
    me = row * 8 + col
    my_text = x * 2 + zl
    my_image = (y * 2 + zh) * 2 + k

    pool_copy = pltpu.make_async_copy(patches, pool.at[pl.ds(0, ROWS)], pool_sem)
    pool_copy.start()

    barrier = pltpu.get_barrier_semaphore()

    lines = [[device((x + d) % 4, y, z, k) for d in (1, 2, 3)]]
    lines.append([device(x, (y + d) % 4, z, k) for d in (1, 2, 3)])
    lines.append([device(x, y, (z + d) % 4, k) for d in (1, 2, 3)])
    lines.append([device(x, y, z, 1 - k)])
    for line in lines:
        for other in line:
            pl.semaphore_signal(barrier, inc=1, device_id=other, device_id_type=MESH)

    places = lax.broadcasted_iota(jnp.int32, (ROWS, ROWS), 0)
    order = (places == pos_row[...]).astype(jnp.float32).astype(jnp.bfloat16)

    def ordered(ref):
        return dot(order, unit(ref[...])).astype(jnp.bfloat16)

    text_learn, text_refer = ordered(txt_l), ordered(txt_r)
    image_learn, image_refer = ordered(img_l), ordered(img_r)
    texts[my_text, 0:2] = text_learn.reshape(2, HALF, D)
    texts[my_text, 2:4] = text_refer.reshape(2, HALF, D)
    images[my_image, 0:2] = image_learn.reshape(2, HALF, D)
    images[my_image, 2:4] = image_refer.reshape(2, HALF, D)

    pl.semaphore_wait(barrier, 10)

    flags[k * 64 + z * 16 + y * 4 + x] = marks[...]
    flag_parts = [
        flags.at[pl.ds(k * 64 + z * 16 + y * 4 + x, 1)],
        flags.at[pl.ds(k * 64 + z * 16 + y * 4, 4)],
        flags.at[pl.ds(k * 64 + z * 16, 16)],
        flags.at[pl.ds(k * 64, 64)],
    ]

    def send_flags(i):
        for other in lines[i]:
            pltpu.make_async_remote_copy(
                src_ref=flag_parts[i],
                dst_ref=flag_parts[i],
                send_sem=send_sems.at[6],
                recv_sem=flag_sems.at[i],
                device_id=other,
                device_id_type=MESH,
            ).start()

    def flags_here(i):
        part = flags.at[pl.ds(0, (3, 12, 48, 64)[i])]
        pltpu.make_async_remote_copy(
            src_ref=part,
            dst_ref=part,
            send_sem=send_sems.at[6],
            recv_sem=flag_sems.at[i],
            device_id=(row, col),
            device_id_type=MESH,
        ).wait_recv()

    send_flags(0)

    def send(buf, sems, slot, quarter, target, sender):
        part = buf.at[slot, quarter]
        pltpu.make_async_remote_copy(
            src_ref=part,
            dst_ref=part,
            send_sem=send_sems.at[sender],
            recv_sem=sems.at[slot, quarter],
            device_id=target,
            device_id_type=MESH,
        ).start()

    def arrived(buf, sems, slot, quarter):
        part = buf.at[slot, quarter]
        pltpu.make_async_remote_copy(
            src_ref=part,
            dst_ref=part,
            send_sem=send_sems.at[0],
            recv_sem=sems.at[slot, quarter],
            device_id=(row, col),
            device_id_type=MESH,
        ).wait_recv()

    def text_at(dx, dz):
        return ((x + dx) % 4) * 2 + (zl + dz) % 2

    def image_at(dy, dz, dk=0):
        return (((y + dy) % 4) * 2 + (zh + dz) % 2) * 2 + (k + dk) % 2

    z_text, z_image = z_of(zh, 1 - zl), z_of(1 - zh, zl)
    x_next, x_prev, x_pair = (
        device((x + 1) % 4, y, z, k),
        device((x + 3) % 4, y, z, k),
        device(x, y, z_text, k),
    )
    y_next, y_prev, y_pair = (
        device(x, (y + 1) % 4, z, k),
        device(x, (y + 3) % 4, z, k),
        device(x, y, z_image, k),
    )
    sibling = device(x, y, z, 1 - k)

    def send_text(slot, quarter, target):
        send(texts, text_sems, slot, quarter, target, 0)

    def send_image(slot, quarter, target):
        send(images, image_sems, slot, quarter, target, 1)

    def text_here(dx, dz, quarter, *targets):
        arrived(texts, text_sems, text_at(dx, dz), quarter)
        for target in targets:
            send_text(text_at(dx, dz), quarter, target)

    def image_here(dy, dz, quarter, *targets):
        arrived(images, image_sems, image_at(dy, dz), quarter)
        for target in targets:
            send_image(image_at(dy, dz), quarter, target)
        send_image(image_at(dy, dz), quarter, sibling)

    for i in range(4):
        up, down = i, (i + 2) % 4
        send_text(my_text, up, x_next)
        send_image(my_image, up, y_next)
        send_text(my_text, down, x_prev)
        send_image(my_image, down, y_prev)
        send_text(my_text, up, x_pair)
        send_image(my_image, up, y_pair)
        send_image(my_image, up, sibling)

    pool[ROWS] = jnp.zeros((PATCH, D), jnp.bfloat16)
    pool_copy.wait()

    def place(i, carry):
        slots[i] = pool[slot_row[i]]
        return carry

    lax.fori_loop(0, 2 * DEVICES, place, 0)
    own_copy = pltpu.make_async_copy(
        slots.at[pl.ds(2 * me, 2)], batches.at[row * 4 + y, pl.ds(2 * k, 2)], own_sem
    )
    own_copy.start()

    for i, line in enumerate(lines):
        for other in line:
            pl.semaphore_signal(line_sems.at[i], inc=1, device_id=other, device_id_type=MESH)
        pl.semaphore_wait(line_sems.at[i], len(line))

    waiting = patch_order()

    def send_patches(count):
        for dx, dy, dz, dk in waiting[:count]:
            r = ((x + dx) % 4) * 4 + (z + dz) % 4
            c = ((y + dy) % 4) * 2 + (k + dk) % 2
            count_here = 2 - dk
            pltpu.make_async_remote_copy(
                src_ref=slots.at[pl.ds(2 * (r * 8 + c), count_here)],
                dst_ref=batches.at[row * 4 + y, pl.ds(2 * k, count_here)],
                send_sem=send_sems.at[2],
                recv_sem=recv_sems.at[4 * dk],
                device_id=(r, c),
                device_id_type=MESH,
            ).start()
        del waiting[:count]

    flags_here(0)
    send_flags(1)
    send_patches(PACE[0])
    for i in range(2):
        text_here(3, 0, i, x_next)
        image_here(3, 0, i, y_next)
        text_here(1, 0, i + 2, x_prev)
        image_here(1, 0, i + 2, y_prev)
        send_patches(PACE[1])
    for i in range(4):
        text_here(0, 1, i, x_next, x_prev)
        image_here(0, 1, i, y_next, y_prev)
        send_patches(PACE[2])
    for i in range(2):
        text_here(3, 0, i + 2)
        image_here(3, 0, i + 2)
        text_here(1, 0, i)
        image_here(1, 0, i)
    flags_here(1)
    send_flags(2)
    for i in (0, 2, 1, 3):
        text_here(2, 0, i, x_pair)
        image_here(2, 0, i, y_pair)
        send_patches(PACE[3])
    for i in range(4):
        for d in (1, 3, 2):
            text_here(d, 1, i)
            image_here(d, 1, i)
        send_patches(PACE[4])
    for i in range(4):
        for dy in range(4):
            for dz in range(2):
                arrived(images, image_sems, image_at(dy, dz, 1), i)

    flags_here(2)
    send_flags(3)
    text_acc[...] = jnp.zeros_like(text_acc)
    image_acc[...] = jnp.zeros_like(image_acc)

    def pair_tile(step, with_grad):
        text_class = step // 4
        image_class = step // 2 % 2
        image_half = step % 2
        blocks = pl.ds(image_half * 8, 8)
        learn_cols = images[blocks, image_class].reshape(8 * HALF, D)
        logit_l[...] = dot_t(texts[:, text_class].reshape(8 * HALF, D), learn_cols)
        refer_cols = images[blocks, 2 + image_class].reshape(8 * HALF, D)
        logit_r[...] = dot_t(texts[:, 2 + text_class].reshape(8 * HALF, D), refer_cols)

        def one_block(b, total):
            for part in range(2):
                start = pl.multiple_of(b * HALF + part * 48, 16)
                rows = pl.ds(start, 48)
                e_l = jnp.exp2(logit_l[rows, :] * EXP_SCALE)
                e_r = jnp.exp2(logit_r[rows, :] * EXP_SCALE)
                p_l, p_r = e_l + SHIFT, e_r + SHIFT
                if with_grad:
                    slope[rows, :] = (e_l / p_l).astype(jnp.bfloat16)

                def gap(parts_l, parts_r):
                    return jnp.log(product(parts_l) * GROUP_SCALE) - jnp.log(
                        product(parts_r) * GROUP_SCALE
                    )

                across = gap(
                    [p_l[:, 128 * i : 128 * (i + 1)] for i in range(GROUP)],
                    [p_r[:, 128 * i : 128 * (i + 1)] for i in range(GROUP)],
                )
                text_acc[b, text_class, pl.ds(part * 48, 48), :] += across
                total = total + gap(
                    [p_l[8 * i : 8 * (i + 1), :] for i in range(GROUP)],
                    [p_r[8 * i : 8 * (i + 1), :] for i in range(GROUP)],
                )
            return total

        image_acc[image_half, image_class] += lax.fori_loop(
            0, 8, one_block, jnp.zeros((8, 8 * HALF), jnp.float32)
        )
        if with_grad:
            grads[...] += dot(slope[...], learn_cols)

    grads[...] = jnp.zeros_like(grads)

    def with_grad(step, carry):
        pair_tile(step, True)
        return carry

    send_patches(PACE[5])
    lax.fori_loop(0, 2, with_grad, 0)

    def to_text_peers(source, landing, sender, receiver):
        for dx, dz in ((0, 1), (1, 0), (3, 0), (1, 1), (3, 1), (2, 0), (2, 1)):
            slot = text_at(dx, dz)
            pltpu.make_async_remote_copy(
                src_ref=source.at[slot],
                dst_ref=landing.at[my_text],
                send_sem=send_sems.at[sender],
                recv_sem=recv_sems.at[receiver],
                device_id=device(slot // 2, y, z_of(zh, slot % 2), k),
                device_id_type=MESH,
            ).start()

    grad_send[...] = grads[...].reshape(8, HALF, D).astype(jnp.bfloat16)
    to_text_peers(grad_send, grad_recv, 3, 1)

    def without_grad(step, carry):
        pair_tile(step, False)
        return carry

    send_patches(PACE[6])
    lax.fori_loop(2, 5, without_grad, 0)
    send_patches(PACE[7])
    lax.fori_loop(5, 8, without_grad, 0)

    ones = jnp.ones((8, 128), jnp.float32)
    for b in range(8):
        sums = dot_t(ones, text_acc[b].reshape(ROWS, 128), HIGHEST)
        text_send[b, :, 0:ROWS] = sums[0:1]
    to_text_peers(text_send, text_recv, 4, 2)
    for h in range(2):
        for a in range(2):
            image_send[h, :, pl.ds(a * 768, 768)] = jnp.sum(image_acc[h, a], axis=0, keepdims=True)
    for d in range(1, 16):
        slot = (my_image + d) % 16
        pltpu.make_async_remote_copy(
            src_ref=image_send.at[slot // 8],
            dst_ref=image_recv.at[my_image],
            send_sem=send_sems.at[5],
            recv_sem=recv_sems.at[3],
            device_id=device(x, slot // 4, z_of(slot // 2 % 2, zl), slot % 2),
            device_id_type=MESH,
        ).start()
    send_patches(len(waiting))
    text_recv[my_text] = text_send[my_text]
    image_recv[my_image] = image_send[my_image // 8]
    grad_recv[my_text] = grad_send[my_text]

    def all_of(buf, count, sender, receiver):
        part = buf.at[pl.ds(0, count)]
        return pltpu.make_async_remote_copy(
            src_ref=part,
            dst_ref=part,
            send_sem=send_sems.at[sender],
            recv_sem=recv_sems.at[receiver],
            device_id=(row, col),
            device_id_type=MESH,
        )

    own_image = image_learn[0:HALF].astype(jnp.float32)
    cosines = jnp.sum(own_image * text_learn[0:HALF].astype(jnp.float32), axis=1, keepdims=True)
    e = jnp.exp2(cosines * EXP_SCALE)
    as_negative = (e / (e + SHIFT)).astype(jnp.bfloat16).astype(jnp.float32)
    as_positive = -(SHIFT / (e + SHIFT)).astype(jnp.bfloat16).astype(jnp.float32)
    all_of(grad_recv, 7, 3, 1).wait_recv()
    total = (as_positive - as_negative) * own_image
    for b in range(8):
        total = total + grad_recv[b].astype(jnp.float32)
    total = total * 10.0
    own_text = dot(order[0:HALF], txt_l[...])
    length = jnp.sqrt(jnp.sum(own_text * own_text, axis=1, keepdims=True) + EPSILON)
    along = jnp.sum(own_text * total, axis=1, keepdims=True) / (length * length * length)
    result = total / length - own_text * along
    grad_out[...] = lax.dot_general(
        order[0:HALF].astype(jnp.float32),
        result,
        (((0,), (0,)), ((), ())),
        preferred_element_type=jnp.float32,
        precision=HIGHEST,
    )

    diagonal = image_refer.astype(jnp.float32) * text_refer.astype(
        jnp.float32
    ) - image_learn.astype(jnp.float32) * text_learn.astype(jnp.float32)
    score = 20.0 * dot_t(jnp.ones((8, D), jnp.float32), diagonal, HIGHEST)
    all_of(text_recv, 7, 4, 2).wait_recv()
    text_sum = jnp.sum(text_recv[:, :, 0:ROWS], axis=0)
    all_of(image_recv, 15, 5, 3).wait_recv()
    image_sum = jnp.sum(image_recv[...], axis=0)
    wanted = lax.broadcasted_iota(jnp.int32, (768, ROWS), 0)
    place_of = lax.broadcasted_iota(jnp.int32, (768, ROWS), 1)
    base = (my_image % 8) * HALF
    pick_sel = (wanted - base == place_of).astype(jnp.float32)
    pick_uns = ((wanted - base + HALF == place_of) & (place_of >= HALF)).astype(jnp.float32)
    pick_sel = jnp.where(place_of < HALF, pick_sel, 0.0)
    rows8 = lambda v: jnp.broadcast_to(v, (8, v.shape[1]))
    score = score + rows8(text_sum)
    score = score + dot(rows8(image_sum[:, 0:768]), pick_sel, HIGHEST)
    score = score + dot(rows8(image_sum[:, 768:1536]), pick_uns, HIGHEST)
    learn_out[...] = dot(score, order.astype(jnp.float32), HIGHEST)[0:1]

    flags_here(3)
    second = flags[...].reshape(DEVICES, DEVICES)
    names = lax.broadcasted_iota(jnp.int32, (8, DEVICES), 1)
    own_column = (names == me).astype(jnp.float32)
    other_column = (names == me + 1 - 2 * k).astype(jnp.float32)
    source = lax.broadcasted_iota(jnp.int32, (DEVICES, DEVICES), 0)
    target = lax.broadcasted_iota(jnp.int32, (DEVICES, DEVICES), 1)
    by_line = (target % 2) * 64 + (target // 8 % 4) * 16 + (target // 2 % 4) * 4 + target // 32
    sorted_out = (source == by_line).astype(jnp.float32)
    mine = dot(dot_t(own_column, second), sorted_out)
    others = dot(dot_t(other_column, second), sorted_out)
    crowded = mine * others * k.astype(jnp.float32)
    summary[0] = mine - crowded
    summary[1] = crowded
    next_one = ((source == target + 1) & (target % 2 == 0)).astype(jnp.float32)
    doubles = jnp.sum(second * dot(second, next_one), axis=0, keepdims=True)
    summary[2] = jnp.broadcast_to(jnp.sum(doubles, axis=1, keepdims=True), (8, DEVICES))

    def rows_of(count, sender, receiver):
        part = slots.at[pl.ds(0, count)]
        return pltpu.make_async_remote_copy(
            src_ref=part,
            dst_ref=part,
            send_sem=send_sems.at[sender],
            recv_sem=recv_sems.at[receiver],
            device_id=(row, col),
            device_id_type=MESH,
        )

    own_copy.wait()
    rows_of(126, 2, 0).wait_recv()
    exchange = pltpu.make_async_remote_copy(
        src_ref=batches.at[:, 2 * k + 1],
        dst_ref=batches.at[:, 2 * k + 1],
        send_sem=send_sems.at[7],
        recv_sem=recv_sems.at[5],
        device_id=sibling,
        device_id_type=MESH,
    )
    exchange.start()
    rows_of(64, 2, 4).wait_recv()
    exchange.wait_send()
    rows_of(64, 2, 5).wait_recv()

    rows_of(190, 2, 0).wait_send()
    all_of(flags, 127, 6, 0).wait_send()
    all_of(texts, 7, 0, 0).wait_send()
    all_of(images, 15, 1, 0).wait_send()
    all_of(grad_send, 7, 3, 1).wait_send()
    all_of(text_send, 7, 4, 2).wait_send()
    all_of(image_recv, 15, 5, 3).wait_send()


def left_over_kernel(slot_row, patches, landing, pool, slots, sems, line_sems):
    row = lax.axis_index("row")
    col = lax.axis_index("col")
    x, z = row // 4, row % 4
    y, k = col // 2, col % 2
    me = row * 8 + col
    pool_copy = pltpu.make_async_copy(patches, pool.at[pl.ds(0, ROWS)], sems.at[0])
    pool_copy.start()
    barrier = pltpu.get_barrier_semaphore()
    lines = [[device((x + d) % 4, y, z, k) for d in (1, 2, 3)]]
    lines.append([device(x, (y + d) % 4, z, k) for d in (1, 2, 3)])
    lines.append([device(x, y, (z + d) % 4, k) for d in (1, 2, 3)])
    lines.append([device(x, y, z, 1 - k)])
    for line in lines:
        for other in line:
            pl.semaphore_signal(barrier, inc=1, device_id=other, device_id_type=MESH)
    pl.semaphore_wait(barrier, 10)
    for i, line in enumerate(lines):
        for other in line:
            pl.semaphore_signal(line_sems.at[i], inc=1, device_id=other, device_id_type=MESH)
        pl.semaphore_wait(line_sems.at[i], len(line))
    pool[ROWS] = jnp.zeros((PATCH, D), jnp.bfloat16)
    pool_copy.wait()

    def place(i, carry):
        slots[i] = pool[slot_row[i]]
        return carry

    lax.fori_loop(0, DEVICES // 2, place, 0)

    def to_chip(source, target):
        return pltpu.make_async_remote_copy(
            src_ref=slots.at[source],
            dst_ref=landing.at[me],
            send_sem=sems.at[1],
            recv_sem=sems.at[2],
            device_id=target,
            device_id_type=MESH,
        )

    for dx, dy, dz, dk in patch_order()[:63]:
        r, c = ((x + dx) % 4) * 4 + (z + dz) % 4, (y + dy) % 4
        to_chip(r * 4 + c, (r, c * 2 + 1)).start()

    def total(count):
        part = pool.at[pl.ds(0, count)]
        return pltpu.make_async_remote_copy(
            src_ref=part,
            dst_ref=part,
            send_sem=sems.at[1],
            recv_sem=sems.at[2],
            device_id=(row, col),
            device_id_type=MESH,
        )

    @pl.when(k == 0)
    def _():
        to_chip(row * 4 + y, (row, y * 2 + 1)).start()
        total(64).wait_send()

    @pl.when(k == 1)
    def _():
        own = pltpu.make_async_copy(slots.at[row * 4 + y], landing.at[me], sems.at[3])
        own.start()
        total(127).wait_recv()
        own.wait()
        total(63).wait_send()


def on_device(img_learner, img_refer, txt_learner, txt_refer, patches, chosen, trainer_of):
    flat = lax.axis_index("row") * lax.axis_size("col") + lax.axis_index("col")
    offsets = chosen - flat * ROWS
    rows = jnp.arange(ROWS, dtype=jnp.int32)
    entries = jnp.arange(HALF, dtype=jnp.int32)
    hits = offsets[:, None] == rows[None, :]
    selected = jnp.any(hits, axis=0)
    as_selected = jnp.sum(jnp.where(hits, entries[:, None], 0), axis=0)
    before = jnp.sum(((rows[:, None] < rows[None, :]) & ~selected[:, None]).astype(jnp.int32), axis=0)
    position = jnp.where(selected, as_selected, HALF + before).astype(jnp.int32)
    owners = trainer_of[:, 0]
    earlier = (owners[:, None] == owners[None, :]) & (entries[None, :] < entries[:, None])
    targets = 2 * owners + jnp.sum(earlier.astype(jnp.int32), axis=1)
    def row_at(slot):
        wanted = targets[:, None] == slot[None, :]
        return ROWS + jnp.sum(jnp.where(wanted, offsets[:, None] - ROWS, 0), axis=0)

    slot = jnp.arange(2 * DEVICES, dtype=jnp.int32)
    first, other = row_at(slot - slot % 4 + 1), row_at(slot - slot % 4 + 3)
    carried = jnp.where(first < ROWS, first, other)
    plan = jnp.where(slot % 2 == 0, row_at(slot), carried)
    seconds = jnp.arange(1, 2 * DEVICES, 2, dtype=jnp.int32)
    marks = jnp.any(targets[:, None] == seconds[None, :], axis=0).astype(jnp.float32)
    left_over = jnp.where(first < ROWS, other, ROWS)[::4]

    vmem = pl.BlockSpec(memory_space=pltpu.VMEM)
    anywhere = pl.BlockSpec(memory_space=pl.ANY)
    bf16, f32 = jnp.bfloat16, jnp.float32
    learnability, text_grad, batches, summary = pl.pallas_call(
        kernel,
        out_shape=(
            jax.ShapeDtypeStruct((1, ROWS), f32),
            jax.ShapeDtypeStruct((ROWS, D), f32),
            jax.ShapeDtypeStruct((DEVICES // 2, 4, PATCH, D), bf16),
            jax.ShapeDtypeStruct((3, 8, DEVICES), f32),
        ),
        in_specs=[pl.BlockSpec(memory_space=pltpu.SMEM)] + [vmem] * 6 + [anywhere],
        out_specs=(vmem, vmem, anywhere, vmem),
        scratch_shapes=[
            pltpu.VMEM((8, 4, HALF, D), bf16),
            pltpu.VMEM((16, 4, HALF, D), bf16),
            pltpu.VMEM((ROWS + 1, PATCH, D), bf16),
            pltpu.VMEM((2 * DEVICES, PATCH, D), bf16),
            pltpu.VMEM((8 * HALF, 8 * HALF), f32),
            pltpu.VMEM((8 * HALF, 8 * HALF), f32),
            pltpu.VMEM((8 * HALF, 8 * HALF), bf16),
            pltpu.VMEM((8 * HALF, D), f32),
            pltpu.VMEM((8, HALF, D), bf16),
            pltpu.VMEM((8, HALF, D), bf16),
            pltpu.VMEM((8, 2, HALF, 128), f32),
            pltpu.VMEM((2, 2, 8, 8 * HALF), f32),
            pltpu.VMEM((8, 1, 256), f32),
            pltpu.VMEM((8, 1, 256), f32),
            pltpu.VMEM((2, 1, 1536), f32),
            pltpu.VMEM((16, 1, 1536), f32),
            pltpu.SemaphoreType.DMA,
            pltpu.SemaphoreType.DMA,
            pltpu.SemaphoreType.DMA((8, 4)),
            pltpu.SemaphoreType.DMA((16, 4)),
            pltpu.SemaphoreType.DMA((8,)),
            pltpu.SemaphoreType.DMA((6,)),
            pltpu.SemaphoreType.REGULAR((4,)),
            pltpu.VMEM((DEVICES, 1, DEVICES), f32),
            pltpu.SemaphoreType.DMA((4,)),
        ],
        compiler_params=pltpu.CompilerParams(
            collective_id=0, has_side_effects=True, vmem_limit_bytes=60 * 1024 * 1024
        ),
        name="jest",
    )(
        plan,
        marks[None, :],
        position[None, :],
        img_learner,
        img_refer,
        txt_learner,
        txt_refer,
        patches,
    )
    batches = batches.reshape(DEVICES, 2, PATCH, D)
    carried_here, crowded_here = summary[0, 0] > 0, summary[1, 0] > 0
    keep = jnp.stack([jnp.ones_like(carried_here), carried_here], axis=1)[:, :, None, None]
    is_second = jnp.array([False, True])[None, :, None, None]

    def with_left_over():
        extra = pl.pallas_call(
            left_over_kernel,
            out_shape=jax.ShapeDtypeStruct((DEVICES, PATCH, D), bf16),
            in_specs=[pl.BlockSpec(memory_space=pltpu.SMEM), anywhere],
            out_specs=anywhere,
            scratch_shapes=[
                pltpu.VMEM((ROWS + 1, PATCH, D), bf16),
                pltpu.VMEM((DEVICES // 2, PATCH, D), bf16),
                pltpu.SemaphoreType.DMA((4,)),
                pltpu.SemaphoreType.REGULAR((4,)),
            ],
            compiler_params=pltpu.CompilerParams(
                collective_id=1, has_side_effects=True, vmem_limit_bytes=32 * 1024 * 1024
            ),
            name="left_over",
        )(left_over, patches)
        base = jnp.where(keep, batches, 0)
        take = crowded_here[:, None, None, None] & is_second
        return jnp.where(take, extra[:, None], base).reshape(2 * DEVICES, PATCH, D)

    def without_left_over():
        return jnp.where(keep, batches, 0).reshape(2 * DEVICES, PATCH, D)

    routed = lax.cond(summary[2, 0, 0] > 0, with_left_over, without_left_over)
    return (learnability[0], text_grad, routed)


def solution(mesh):
    placed = (
        P(("row", "col"), None),
        P(("row", "col"), None),
        P(("row", "col"), None),
        P(("row", "col"), None),
        P(("row", "col"), None, None),
        P(("row", "col")),
        P(("row", "col"), None),
    )
    return jax.shard_map(
        on_device,
        mesh=mesh,
        in_specs=placed,
        out_specs=(P(("row", "col")), P(("row", "col"), None), P(("row", "col"), None, None)),
        check_vma=False,
    )
```
